256 devices in a mesh: seq: 32 (over x, y, core), ch: 8 (over z).
Axes of the slice: x: 4, y: 4, z: 8, core: 2. Of those that a mesh axis runs over, the one named last changes fastest.
Arguments:
- query_in: bfloat16 [16384, 8192], P('seq', 'ch'), may hold values from -6 to 6
- key_in: bfloat16 [16384, 8192], P('seq', 'ch'), may hold values from -6 to 6
- value_in: bfloat16 [16384, 8192], P('seq', 'ch'), may hold values from -6 to 6
- short_weight: float32 [3, 3, 8192], P(None, None, 'ch'), may hold values from -3 to 3
- skip_bias: float32 [8192], P('ch'), may hold values from -4 to 4
- filter_taps: float32 [512, 16384], P('ch', 'seq'), may hold values from -0.046875 to 0.046875
Outputs:
- hyena_out: bfloat16 [16384, 8192], P('seq', 'ch')
The draws below stay inside these ranges and needn't reach their ends.
All inputs are finite; a program needn't handle non-finite values.
Results may differ from the reference program's by a relative error of at most 0.001.
Values may be sent and summed in bfloat16 or wider, within the bound.
No kernel may reach another device: no remote copies, remote signals or barrier semaphores. Data moves between devices by JAX's collectives and lax.ppermute only.
A program may use at most 192 MiB of HBM per device.

```python
import jax
import jax.numpy as jnp
from jax import lax

D = 8192
GROUP_SIZE = 16
TOKENS = 16384
GROUPS = 512


def level_of(own_key, extent, cuts, smallest, largest):
    level, own = 1.0, jax.random.fold_in(own_key, 6)
    for axis_at, parts in cuts:
        steps = jnp.exp(jax.random.uniform(jax.random.fold_in(own, axis_at), (parts,), jnp.float32, smallest / len(cuts), largest / len(cuts)))
        level = level * jnp.repeat(steps, extent[axis_at] // parts).reshape([-1 if axis == axis_at else 1 for axis in range(len(extent))])
    return level


def centred(own_key, shape, scale, most, split=(), kind=jnp.bfloat16):
    drawn = jax.random.normal(own_key, shape, jnp.float32) * scale
    if len(split) > 0:
        drawn = level_of(own_key, shape, split, -0.22, 0.18) * drawn
    return jnp.clip(drawn, min=-most, max=most).astype(kind)


def setup_inputs(seed: int = 0) -> dict:
    key_list = jax.random.split(jax.random.key(seed), 7)
    return {
        "query_in": centred(key_list[0], (TOKENS, D), 1.0, 6.0, ((0, 32), (1, 8))),
        "key_in": centred(key_list[1], (TOKENS, D), 1.0, 6.0, ((0, 32), (1, 8))),
        "value_in": centred(key_list[2], (TOKENS, D), 1.0, 6.0, ((0, 32), (1, 8))),
        "short_weight": centred(key_list[3], (3, 3, D), 0.6, 3.0, ((2, 8),), jnp.float32),
        "skip_bias": centred(key_list[4], (D,), 1.0, 4.0, ((0, 8),), jnp.float32),
        "filter_taps": centred(key_list[5], (GROUPS, TOKENS), TOKENS ** -0.5, 0.046875, ((0, 8), (1, 32)), jnp.float32),
    }


def short_conv(stream, weights):
    padded = jnp.pad(stream.astype(jnp.float32), ((2, 0), (0, 0)))
    return weights[0] * padded[2:] + weights[1] * padded[1:-1] + weights[2] * padded[:-2]


def one_group(pieces):
    query_block, key_block, value_block, weights, bias_block, taps = pieces
    seq_length = query_block.shape[0]
    q_short = short_conv(query_block, weights[0])
    k_short = short_conv(key_block, weights[1])
    v_short = short_conv(value_block, weights[2])
    gated_product = k_short * v_short
    signal_spectrum = jnp.fft.rfft(gated_product, n=2 * seq_length, axis=0)
    filter_spectrum = jnp.fft.rfft(taps, n=2 * seq_length)
    long_conv = jnp.fft.irfft(signal_spectrum * filter_spectrum[:, None], n=2 * seq_length, axis=0)[:seq_length]
    return (q_short * (long_conv + bias_block * gated_product)).astype(jnp.bfloat16)


def reference(query_in, key_in, value_in, short_weight, skip_bias, filter_taps):
    seq_length = query_in.shape[0]

    def by_group(stream):
        return stream.reshape(seq_length, GROUPS, GROUP_SIZE).transpose(1, 0, 2)

    weights = short_weight.reshape(3, 3, GROUPS, GROUP_SIZE).transpose(2, 0, 1, 3)
    outputs = lax.map(one_group, (by_group(query_in), by_group(key_in), by_group(value_in), weights, skip_bias.reshape(GROUPS, GROUP_SIZE), filter_taps))
    return outputs.transpose(1, 0, 2).reshape(seq_length, D)
```

```python
import math

import jax
import jax.numpy as jnp
import numpy as np
from jax import lax
from jax.experimental import pallas as pl
from jax.experimental.pallas import tpu as pltpu
from jax.sharding import PartitionSpec as P

GROUP_SIZE = 16
SIDE = 128
LANES = 128
CODE_SPAN = 240.0
CODE_TOP = 4096.0
CODE_GAIN = CODE_SPAN / math.log2(1.0 + CODE_TOP)
INV_LN2 = 1.0 / math.log(2.0)
VMEM_LIMIT = 48 * 1024 * 1024

f32, bf16 = jnp.float32, jnp.bfloat16


def encode(value, to_units):
    level = jnp.log(1.0 + jnp.abs(value) * to_units) * (CODE_GAIN * INV_LN2)
    code = jnp.exp2(level - CODE_SPAN / 2)
    return jnp.where(value < 0, -code, code)


def decode(code, from_units):
    level = jnp.log(jnp.abs(code)) * (INV_LN2 / CODE_GAIN)
    size = (jnp.exp2(level + CODE_SPAN / 2 / CODE_GAIN) - 1.0) * from_units
    return jnp.where(code < 0, -size, size)


def code_scale(largest):
    return (jnp.maximum(largest, 1e-30) * 1.01).astype(bf16).astype(f32)


def tables():
    side = np.arange(SIDE)
    inner = 2 * np.pi / SIDE * (side[:, None] * side[None, :] % SIDE)
    outer = 2 * np.pi / (4 * SIDE) * (side[None, :] * (4 * side[:, None] + 1) % (4 * SIDE))
    twist = 2 * np.pi / (4 * SIDE * SIDE) * (side[None, :] * (4 * side[:, None] + 1))
    first = np.concatenate([np.cos(outer), -np.sin(outer)], axis=0)
    second = np.block([[np.cos(inner), -np.sin(inner)], [np.sin(inner), np.cos(inner)]])
    third = np.block([[np.cos(inner), np.sin(inner)], [-np.sin(inner), np.cos(inner)]])
    fourth = np.concatenate([np.cos(outer).T, -np.sin(outer).T], axis=1)

    def parts(table):
        high = table.astype(jnp.bfloat16)
        low = (table - high.astype(np.float64)).astype(jnp.bfloat16)
        return np.stack([high, low])

    return (
        parts(first),
        parts(second),
        parts(third),
        parts(fourth),
        np.stack([np.cos(twist), np.sin(twist)]).astype(np.float32),
    )


def dot(left, right):
    return jnp.dot(left, right, preferred_element_type=f32)


def halves(value):
    high = value.astype(bf16)
    return high, (value - high.astype(f32)).astype(bf16)


def table_left(table, value):
    high, low = halves(value)
    return dot(table[0], high) + dot(table[1], high) + dot(table[0], low)


def table_right(value, table):
    high, low = halves(value)
    return dot(high, table[0]) + dot(low, table[0]) + dot(high, table[1])


def short_conv(stream, edge, weights, padded):
    rows = stream.shape[0]
    padded[6:8, :] = edge.astype(f32)
    padded[8 : 8 + rows, :] = stream.astype(f32)
    return (
        weights[0:1] * padded[8 : 8 + rows, :]
        + weights[1:2] * padded[7 : 7 + rows, :]
        + weights[2:3] * padded[6 : 6 + rows, :]
    )


def gate_kernel(k_ref, v_ref, edge_ref, w_ref, taps_ref, out_ref, k_pad, v_pad, taps_in, taps_pad):
    rows = k_ref.shape[0]
    dests = out_ref.shape[0]
    per = LANES // dests
    k_short = short_conv(k_ref[...], edge_ref[1], w_ref[1], k_pad)
    v_short = short_conv(v_ref[...], edge_ref[2], w_ref[2], v_pad)
    gated = k_short * v_short
    scale = code_scale(jnp.max(jnp.abs(gated), axis=0, keepdims=True))
    code = encode(gated, CODE_TOP / scale)
    for a in range(rows // SIDE):
        tile = code[a * SIDE : (a + 1) * SIDE, :].T.astype(bf16)
        out_ref[:, a * per : (a + 1) * per, :] = tile.reshape(dests, per, LANES)
    groups = taps_ref.shape[0] // dests
    base = rows // SIDE * per
    held = taps_ref.shape[0]
    for a in range(rows // SIDE):
        taps_in[a * held : (a + 1) * held, :] = taps_ref[:, a * LANES : (a + 1) * LANES]
    for a in range(rows // SIDE):
        for g in range(groups):
            piece = taps_in[pl.ds(a * held + g, dests, stride=groups), :]
            taps_pad[pl.ds(a * groups + g, dests, stride=8), :] = piece
    high, low = halves(taps_pad[...].reshape(dests, 8, LANES))
    out_ref[:, base : base + 16, :] = jnp.concatenate(
        [high.astype(f32), low.astype(f32)], axis=1
    ).astype(bf16)
    extra = jnp.concatenate(
        [
            jnp.broadcast_to(pltpu.roll(scale, (LANES - d * per) % LANES, 1), (8, LANES))[None]
            for d in range(dests)
        ],
        axis=0,
    )
    out_ref[:, base + 16 : base + 24, :] = extra.astype(bf16)


def mix_kernel(
    in_ref, first, second, third, fourth, twist, out_ref, signal, taps, result, spectra, scales
):
    blocks = in_ref.shape[0]
    per_block = SIDE // blocks
    data = signal.shape[0] // blocks
    channels = data // per_block
    groups = channels // GROUP_SIZE
    lane = lax.broadcasted_iota(jnp.int32, (channels, LANES), 1)
    row = lax.broadcasted_iota(jnp.int32, (channels, LANES), 0)
    ones = jnp.ones((LANES, LANES), bf16)

    def unpack(j, carry):
        tail = in_ref[j, data : data + 24, :].astype(f32)
        scale_row = tail[16:17, :] * (1.0 / CODE_TOP)
        picked = jnp.where(lane == row, scale_row, 0.0).astype(bf16)
        scale = dot(picked, ones)
        value = decode(
            in_ref[j, 0:data, :].astype(f32).reshape(per_block, channels, LANES), scale[None]
        )
        signal[pl.ds(pl.multiple_of(j * data, data), data), :] = value.reshape(data, LANES)
        taps[pl.ds(pl.multiple_of(j * 8, 8), 8), :] = tail[0:8] + tail[8:16]
        return carry

    lax.fori_loop(0, blocks, unpack, 0, unroll=2)

    cos, sin = twist[0], twist[1]

    def forward(values):
        wide = table_left(first, jnp.concatenate(values, axis=1))
        turned = []
        for at in range(len(values)):
            re = wide[:SIDE, at * SIDE : (at + 1) * SIDE]
            im = wide[SIDE:, at * SIDE : (at + 1) * SIDE]
            turned.append(jnp.concatenate([re * cos + im * sin, im * cos - re * sin], axis=1))
        return table_right(jnp.concatenate(turned, axis=0), second)

    found = forward([taps[pl.ds(g, SIDE, stride=groups), :] for g in range(groups)])
    spectra[...] = found.reshape(groups, SIDE, 2 * SIDE) * (1.0 / (SIDE * SIDE))
    scales[...] = jnp.zeros_like(scales)

    def pair(at):
        spectrum = forward([signal[pl.ds(at + i, SIDE, stride=channels), :] for i in range(2)])
        spectrum = spectrum.reshape(2, SIDE, 2 * SIDE)
        taps_spectrum = spectra[at // GROUP_SIZE]
        f_re, f_im = taps_spectrum[None, :, :SIDE], taps_spectrum[None, :, SIDE:]
        s_re, s_im = spectrum[:, :, :SIDE], spectrum[:, :, SIDE:]
        product = jnp.concatenate([s_re * f_re - s_im * f_im, s_re * f_im + s_im * f_re], axis=2)
        back = table_right(product.reshape(2 * SIDE, 2 * SIDE), third)
        turned = []
        for i in range(2):
            re = back[i * SIDE : (i + 1) * SIDE, :SIDE]
            im = back[i * SIDE : (i + 1) * SIDE, SIDE:]
            turned.append(jnp.concatenate([re * cos - im * sin, im * cos + re * sin], axis=0))
        done = table_left(fourth, jnp.concatenate(turned, axis=1))
        largest = jnp.max(jnp.abs(done), axis=0, keepdims=True)
        for i in range(2):
            result[pl.ds(at + i, SIDE, stride=channels), :] = done[:, i * SIDE : (i + 1) * SIDE]
            top = jnp.max(largest[:, i * SIDE : (i + 1) * SIDE], axis=1, keepdims=True)
            scales[pl.ds(at + i, 1), :] = jnp.broadcast_to(top, (1, LANES))

    def step(n, carry):
        pair(4 * n)
        pair(4 * n + 2)
        return carry

    lax.fori_loop(0, channels // 4, step, 0)

    scale = code_scale(scales[...])
    to_units = CODE_TOP / scale
    scale_row = jnp.sum(jnp.where(lane == row, scale, 0.0), axis=0, keepdims=True)
    tail = jnp.broadcast_to(scale_row, (8, LANES)).astype(bf16)

    def pack(j, carry):
        value = result[pl.ds(pl.multiple_of(j * data, data), data), :]
        code = encode(value.reshape(per_block, channels, LANES), to_units[None])
        out_ref[j, 0:data, :] = code.reshape(data, LANES).astype(bf16)
        out_ref[j, data : data + 8, :] = tail
        return carry

    lax.fori_loop(0, blocks, pack, 0, unroll=2)


def local_kernel(
    q_ref, k_ref, v_ref, edge_ref, w_ref, skip_ref, q_out, s_out, q_pad, k_pad, v_pad
):
    q_short = short_conv(q_ref[...], edge_ref[0], w_ref[0], q_pad)
    k_short = short_conv(k_ref[...], edge_ref[1], w_ref[1], k_pad)
    v_short = short_conv(v_ref[...], edge_ref[2], w_ref[2], v_pad)
    q_out[...] = q_short
    s_out[...] = skip_ref[...] * (k_short * v_short)


def join_kernel(in_ref, q_ref, s_ref, out_ref):
    rows = q_ref.shape[0]
    sources = in_ref.shape[0]
    per = LANES // sources
    base = rows // SIDE * per
    lane = lax.broadcasted_iota(jnp.int32, (1, LANES), 1)
    scale = jnp.zeros((1, LANES), f32)
    for i in range(sources):
        row = pltpu.roll(in_ref[i, base : base + 8, :].astype(f32)[0:1], i * per, 1)
        scale = jnp.where(lane // per == i, row, scale)
    from_units = scale * (1.0 / CODE_TOP)
    for a in range(rows // SIDE):
        tile = in_ref[:, a * per : (a + 1) * per, :].astype(f32).reshape(LANES, SIDE).T
        span = slice(a * SIDE, (a + 1) * SIDE)
        long_conv = decode(tile, from_units)
        out_ref[span, :] = (q_ref[span, :] * (long_conv + s_ref[span, :])).astype(bf16)


def shards(query_in, key_in, value_in, short_weight, skip_bias, filter_taps):
    rows, channels = query_in.shape
    seq = lax.axis_size("seq")
    own = channels // seq
    blocks = channels // LANES
    dests = LANES // own
    groups = filter_taps.shape[0] // blocks
    sent = rows * own // LANES
    edge = lax.ppermute(
        jnp.stack([query_in[-2:], key_in[-2:], value_in[-2:]]),
        "seq",
        [(at, at + 1) for at in range(seq - 1)],
    )
    params = pltpu.CompilerParams(vmem_limit_bytes=VMEM_LIMIT)

    stream = pl.BlockSpec((rows, LANES), lambda b: (0, b))
    edge_spec = pl.BlockSpec((3, 2, LANES), lambda b: (0, 0, b))
    weight_spec = pl.BlockSpec((3, 3, LANES), lambda b: (0, 0, b))
    pad = pltpu.VMEM((rows + 8, LANES), f32)

    message = pl.pallas_call(
        gate_kernel,
        grid=(blocks,),
        in_specs=[
            stream,
            stream,
            edge_spec,
            weight_spec,
            pl.BlockSpec((groups, rows), lambda b: (b, 0)),
        ],
        out_specs=pl.BlockSpec((dests, sent + 24, LANES), lambda b: (b, 0, 0)),
        out_shape=jax.ShapeDtypeStruct((seq, sent + 24, LANES), bf16),
        scratch_shapes=[
            pad,
            pad,
            pltpu.VMEM((groups * rows // LANES, LANES), f32),
            pltpu.VMEM((dests * 8, LANES), f32),
        ],
        compiler_params=params,
        name="gate",
    )(key_in, value_in, edge, short_weight, filter_taps)
    message = lax.all_to_all(message, "seq", 0, 0)

    q_short, skipped = pl.pallas_call(
        local_kernel,
        grid=(blocks,),
        in_specs=[
            stream,
            stream,
            stream,
            edge_spec,
            weight_spec,
            pl.BlockSpec((1, LANES), lambda b: (0, b)),
        ],
        out_specs=[stream, stream],
        out_shape=[jax.ShapeDtypeStruct((rows, channels), f32)] * 2,
        scratch_shapes=[pad, pad, pad],
        compiler_params=params,
        cost_estimate=pl.CostEstimate(
            flops=20 * rows * channels, bytes_accessed=14 * rows * channels, transcendentals=0
        ),
        name="local",
    )(query_in, key_in, value_in, edge, short_weight, skip_bias[None])

    whole = pl.BlockSpec(memory_space=pltpu.VMEM)
    message = pl.pallas_call(
        mix_kernel,
        in_specs=[whole] * 6,
        out_specs=whole,
        out_shape=jax.ShapeDtypeStruct((seq, sent + 8, LANES), bf16),
        scratch_shapes=[
            pltpu.VMEM((seq * sent, LANES), f32),
            pltpu.VMEM((seq * 8, LANES), f32),
            pltpu.VMEM((seq * sent, LANES), f32),
            pltpu.VMEM((own // GROUP_SIZE, SIDE, 2 * SIDE), f32),
            pltpu.VMEM((own, LANES), f32),
        ],
        compiler_params=params,
        name="mix",
    )(message, *tables())
    message = lax.all_to_all(message, "seq", 0, 0)

    return pl.pallas_call(
        join_kernel,
        grid=(blocks,),
        in_specs=[
            pl.BlockSpec((dests, sent + 8, LANES), lambda b: (b, 0, 0)),
            stream,
            stream,
        ],
        out_specs=stream,
        out_shape=jax.ShapeDtypeStruct((rows, channels), bf16),
        compiler_params=params,
        name="join",
    )(message, q_short, skipped)


def solution(mesh):
    in_specs = (
        P("seq", "ch"),
        P("seq", "ch"),
        P("seq", "ch"),
        P(None, None, "ch"),
        P("ch"),
        P("ch", "seq"),
    )
    out_specs = P("seq", "ch")
    return jax.shard_map(shards, mesh=mesh, in_specs=in_specs, out_specs=out_specs, check_vma=False)
```

```python
import math

import jax
import jax.numpy as jnp
import numpy as np
from jax import lax
from jax.experimental import pallas as pl
from jax.experimental.pallas import tpu as pltpu
from jax.sharding import PartitionSpec as P

GROUP_SIZE = 16
SIDE = 128
LANES = 128
WIDE = 4
CODE_SPAN = 240.0
CODE_TOP = 4096.0
CODE_GAIN = CODE_SPAN / math.log2(1.0 + CODE_TOP)
INV_LN2 = 1.0 / math.log(2.0)
RESIDENT_LIMIT = 12 * 1024 * 1024
STREAMING_LIMIT = 60 * 1024 * 1024

f32, bf16 = jnp.float32, jnp.bfloat16


def encode(value, to_units):
    level = jnp.log(1.0 + jnp.abs(value) * to_units) * (CODE_GAIN * INV_LN2)
    code = jnp.exp2(level - CODE_SPAN / 2)
    return jnp.where(value < 0, -code, code)


def decode(code, from_units):
    level = jnp.log(jnp.abs(code)) * (INV_LN2 / CODE_GAIN)
    size = (jnp.exp2(level + CODE_SPAN / 2 / CODE_GAIN) - 1.0) * from_units
    return jnp.where(code < 0, -size, size)


def code_scale(largest):
    return (jnp.maximum(largest, 1e-30) * 1.01).astype(bf16).astype(f32)


def tables():
    side = np.arange(SIDE)
    inner = 2 * np.pi / SIDE * (side[:, None] * side[None, :] % SIDE)
    outer = 2 * np.pi / (4 * SIDE) * (side[None, :] * (4 * side[:, None] + 1) % (4 * SIDE))
    twist = 2 * np.pi / (4 * SIDE * SIDE) * (side[None, :] * (4 * side[:, None] + 1))
    first = np.concatenate([np.cos(outer), -np.sin(outer)], axis=0)
    second = np.block([[np.cos(inner), -np.sin(inner)], [np.sin(inner), np.cos(inner)]])
    third = np.block([[np.cos(inner), np.sin(inner)], [-np.sin(inner), np.cos(inner)]])
    fourth = np.concatenate([np.cos(outer).T, -np.sin(outer).T], axis=1)

    def parts(table):
        high = table.astype(jnp.bfloat16)
        return high, (table - high.astype(np.float64)).astype(jnp.bfloat16)

    def beside(table):
        high, low = parts(table)
        return np.concatenate([high, high, low], axis=0)

    return (
        np.concatenate([np.concatenate([part, part], axis=1) for part in parts(first)], axis=0),
        beside(second),
        beside(third),
        np.concatenate(parts(fourth), axis=0),
        np.stack([np.cos(twist), np.sin(twist)]).astype(np.float32),
    )


def dot(left, right):
    return jnp.dot(left, right, preferred_element_type=f32)


def halves(value):
    high = value.astype(bf16)
    return high, (value - high.astype(f32)).astype(bf16)


def short_conv(stream, at, lanes, before, weights, padded):
    now = stream[pl.ds(at, SIDE), lanes].astype(f32)
    padded[8:16, :] = before
    padded[16:, :] = now
    return (
        weights[0:1] * now
        + weights[1:2] * padded[15 : 15 + SIDE, :]
        + weights[2:3] * padded[14 : 14 + SIDE, :]
    )


def gate_kernel(
    q_hbm,
    k_hbm,
    v_hbm,
    w_hbm,
    taps_hbm,
    out_hbm,
    k_buf,
    v_buf,
    q_buf,
    w_buf,
    taps_buf,
    out_ref,
    pads,
    scales,
    ends,
    q_ends,
    taps_in,
    sems,
):
    rows, channels = k_buf.shape
    steps = rows // SIDE
    blocks = channels // LANES
    dests = out_ref.shape[0] // blocks
    per = LANES // dests
    base = steps * per
    held = taps_buf.shape[0] // blocks
    groups = held // dests

    def stream_copy(at, step):
        source, target = ((k_hbm, k_buf), (v_hbm, v_buf))[at]
        span = pl.ds(step * SIDE, SIDE)
        return pltpu.make_async_copy(source.at[span], target.at[span], sems.at[at, step])

    def out_copy(step):
        end = base + 16 if step == steps - 1 else (step + 1) * per
        span = pl.ds(step * per, end - step * per)
        return pltpu.make_async_copy(out_ref.at[:, span], out_hbm.at[:, span], sems.at[3, step])

    w_copy = pltpu.make_async_copy(w_hbm, w_buf, sems.at[2, 0])
    taps_copy = pltpu.make_async_copy(taps_hbm, taps_buf, sems.at[2, 1])
    q_copy = pltpu.make_async_copy(q_hbm.at[pl.ds(rows - 16, 16)], q_buf, sems.at[2, 2])
    for step in range(steps):
        for at in range(2):
            stream_copy(at, step).start()
        if step == 0:
            w_copy.start()
    taps_copy.start()
    q_copy.start()
    w_copy.wait()

    for step in range(steps):
        for at in range(2):
            stream_copy(at, step).wait()

        def tile(block, slot, step=step):
            lanes = pl.ds(pl.multiple_of(block * LANES, LANES), LANES)
            shorts = []
            for at, buf in enumerate((k_buf, v_buf)):
                if step == 0:
                    before = jnp.zeros((8, LANES), f32)
                else:
                    before = buf[step * SIDE - 16 : step * SIDE, lanes].astype(f32)[8:]
                shorts.append(
                    short_conv(
                        buf, step * SIDE, lanes, before, w_buf[1 + at, :, lanes], pads.at[slot, at]
                    )
                )
            gated = shorts[0] * shorts[1]
            scale = code_scale(jnp.max(jnp.abs(gated), axis=0, keepdims=True))
            scales[step : step + 1, lanes] = scale
            code = encode(gated, CODE_TOP / scale).T.astype(bf16)
            first = pl.multiple_of(block * dests, dests)
            out_ref[pl.ds(first, dests), step * per : (step + 1) * per, :] = code.reshape(
                dests, per, LANES
            )

        def tiles(n, carry):
            tile(2 * n, 0)
            tile(2 * n + 1, 1)
            return carry

        lax.fori_loop(0, blocks // 2, tiles, 0)
        if step < steps - 1:
            out_copy(step).start()

    taps_copy.wait()
    q_copy.wait()

    def tail(block, slot):
        lanes = pl.ds(pl.multiple_of(block * LANES, LANES), LANES)
        for a in range(steps):
            taps_in[slot, a * held : (a + 1) * held, :] = taps_buf[
                pl.ds(pl.multiple_of(block * held, held), held), a * LANES : (a + 1) * LANES
            ]
        taps_at = steps * held
        for a in range(steps):
            for g in range(groups):
                piece = taps_in[slot, pl.ds(a * held + g, dests, stride=groups), :]
                taps_in[slot, pl.ds(taps_at + a * groups + g, dests, stride=8), :] = piece
        own_taps = taps_in[slot, taps_at:, :]
        taps_scale = code_scale(jnp.max(jnp.abs(own_taps), axis=1, keepdims=True))
        taps_code = encode(own_taps, CODE_TOP / taps_scale)
        taps_scale = jnp.broadcast_to(taps_scale, own_taps.shape)
        for at, buf in enumerate((k_buf, v_buf)):
            ends[slot, 4 * at : 4 * at + 2, :] = buf[rows - 16 :, lanes].astype(f32)[14:16]
            ends[slot, 4 * at + 2 : 4 * at + 4, :] = buf[0:16, lanes].astype(f32)[0:2]
        q_ends[slot, 0:2, :] = q_buf[:, lanes].astype(f32)[14:16]
        lane = lax.broadcasted_iota(jnp.int32, (8, LANES), 1)
        for d in range(dests):
            asked = pltpu.roll(q_ends[slot], (LANES + 3 * per - d * per) % LANES, 1)
            kept = pltpu.roll(ends[slot], (LANES - d * per) % LANES, 1)
            scaled = pltpu.roll(scales[:, lanes], (LANES + per - d * per) % LANES, 1)
            of_taps = taps_scale[8 * d : 8 * d + 8]
            last = jnp.where(lane < per, kept, jnp.where(lane < 2 * per, scaled, of_taps))
            last = jnp.where(lane < 3 * per, last, asked)
            both = jnp.concatenate([taps_code[8 * d : 8 * d + 8], last], axis=0).astype(bf16)
            out_ref[block * dests + d, base : base + 16, :] = both

    def tails(n, carry):
        tail(2 * n, 0)
        tail(2 * n + 1, 1)
        return carry

    scales[steps:, :] = jnp.zeros((8 - steps, channels), f32)
    q_ends[...] = jnp.zeros_like(q_ends)
    lax.fori_loop(0, blocks // 2, tails, 0)
    out_copy(steps - 1).start()
    for step in range(steps):
        out_copy(step).wait()


def mix_kernel(
    in_hbm,
    w_hbm,
    first_hbm,
    second_hbm,
    third_hbm,
    fourth_hbm,
    twist_hbm,
    out_hbm,
    in_ref,
    w_ref,
    first,
    second,
    third,
    fourth,
    twist,
    out_ref,
    signal_0,
    signal_1,
    result_0,
    result_1,
    taps,
    spectra,
    largest,
    units,
    tails,
    back_tails,
    levels,
    starts,
    turned,
    filtered,
    unturned,
    in_sems,
    table_sems,
    out_sems,
):
    signals, results = (signal_0, signal_1), (result_0, result_1)
    groups = len(signals)
    blocks = in_ref.shape[0]
    per_block = SIDE // blocks
    channels = groups * GROUP_SIZE
    data = per_block * channels
    count = channels // WIDE
    slots = count // groups
    slot_blocks = blocks // slots

    def in_copy(slot):
        span = pl.ds(slot * slot_blocks, slot_blocks)
        return pltpu.make_async_copy(in_hbm.at[span], in_ref.at[span], in_sems.at[slot])

    def out_copy(slot):
        span = pl.ds(slot * slot_blocks, slot_blocks)
        return pltpu.make_async_copy(out_ref.at[span], out_hbm.at[span], out_sems.at[slot])

    table_copies = [
        pltpu.make_async_copy(source, target, table_sems.at[at])
        for at, (source, target) in enumerate(
            (
                (w_hbm, w_ref),
                (twist_hbm, twist),
                (first_hbm, first),
                (second_hbm, second),
                (third_hbm, third),
                (fourth_hbm, fourth),
            )
        )
    ]
    for slot in range(slots):
        in_copy(slot).start()
    for copy in table_copies:
        copy.start()

    lane = lax.broadcasted_iota(jnp.int32, (GROUP_SIZE, LANES), 1)

    def start_of(j, group):
        return starts[j * channels + group * GROUP_SIZE : j * channels + (group + 1) * GROUP_SIZE, :]

    def unpack(slot, group, with_starts):
        for i in range(slot_blocks):
            j = slot * slot_blocks + i
            for a in range(per_block):
                at = a * channels + group * GROUP_SIZE
                value = decode(in_ref[j, at : at + GROUP_SIZE, :].astype(f32), 1.0)
                if a == 0 and with_starts:
                    value = jnp.where(lane < 2, start_of(j, group), value)
                place = (j * per_block + a) * GROUP_SIZE
                signals[group][place : place + GROUP_SIZE, :] = value

    for slot in range(slots):
        in_copy(slot).wait()
        unpack(slot, 0, False)
    table_copies[0].wait()

    of_message = in_ref[:, data : data + 16, :].astype(f32)
    tails[...] = of_message[:, 8:].reshape(blocks * 8, LANES)
    taps_code = of_message[:, :8].reshape(blocks * 8, LANES)
    taps[...] = decode(taps_code, 1.0 / CODE_TOP) * tails[:, 2 * channels : 2 * channels + 1]
    for a in range(per_block):
        levels[pl.ds(a, blocks, stride=per_block), :] = tails[pl.ds(a, blocks, stride=8), :]

    def gated_starts():
        block = lax.broadcasted_iota(jnp.int32, (blocks, LANES), 0)
        lanes = lax.broadcasted_iota(jnp.int32, (blocks, LANES), 1)
        shorts = []
        for at in range(2):
            ago_2, ago_1, now, later = [
                tails[pl.ds(4 * at + i, blocks, stride=8), :] for i in range(4)
            ]
            ago_2 = jnp.where(block == 0, 0.0, pltpu.roll(ago_2, 1, 0))
            ago_1 = jnp.where(block == 0, 0.0, pltpu.roll(ago_1, 1, 0))
            back_tails[pl.ds(3 + 2 * at, blocks, stride=8), :] = ago_2
            back_tails[pl.ds(4 + 2 * at, blocks, stride=8), :] = ago_1
            taps_0, taps_1, taps_2 = [w_ref[1 + at, i : i + 1, :] for i in range(3)]
            shorts.append(
                (
                    taps_0 * now + taps_1 * ago_1 + taps_2 * ago_2,
                    taps_0 * later + taps_1 * now + taps_2 * ago_1,
                )
            )
        for at in range(2):
            asked = pltpu.roll(tails[pl.ds(at, blocks, stride=8), :], LANES - 3 * channels, 1)
            asked = jnp.where(block == 0, 0.0, pltpu.roll(asked, 1, 0))
            back_tails[pl.ds(1 + at, blocks, stride=8), :] = asked
        level = pltpu.roll(tails[pl.ds(0, blocks, stride=8), :], LANES - channels, 1)
        to_level = CODE_TOP / jnp.where(lanes < channels, level, 1.0)
        packed = jnp.zeros((blocks, LANES), f32)
        for token in range(2):
            parts = halves(shorts[0][token] * shorts[1][token] * to_level)
            for at, part in enumerate(parts):
                place = 2 * token + at
                moved = pltpu.roll(part.astype(f32), place * channels, 1)
                packed = jnp.where(lanes // channels == place, moved, packed)
        lane = lax.broadcasted_iota(jnp.int32, (blocks, channels, LANES), 2)
        row = lax.broadcasted_iota(jnp.int32, (blocks, channels, LANES), 1)
        picked = jnp.where(lane % channels == row, packed[:, None, :], 0.0).astype(bf16)
        from_lane = lax.broadcasted_iota(jnp.int32, (LANES, LANES), 0)
        to_lane = lax.broadcasted_iota(jnp.int32, (LANES, LANES), 1)
        place = jnp.where(from_lane // (2 * channels) == to_lane, 1.0, 0.0).astype(bf16)
        starts[...] = dot(picked.reshape(blocks * channels, LANES), place)

    gated_starts()
    for j in range(blocks):
        place = j * per_block * GROUP_SIZE
        span = slice(place, place + GROUP_SIZE)
        signal_0[span, :] = jnp.where(lane < 2, start_of(j, 0), signal_0[span, :])
    for copy in table_copies[1:]:
        copy.wait()

    cos, sin = twist[0], twist[1]

    def store_halves(ref, at, value):
        high, low = halves(value)
        ref[at * SIDE : (at + 1) * SIDE, : 2 * SIDE] = high
        ref[at * SIDE : (at + 1) * SIDE, 2 * SIDE :] = low

    def table_right(ref, table, used=WIDE):
        rows = used * SIDE
        return dot(ref[:rows], table[: 4 * SIDE]) + dot(ref[:rows, : 2 * SIDE], table[4 * SIDE :])

    def first_side(values):
        for pair in range(len(values) // 2):
            high, low = halves(jnp.concatenate(values[2 * pair : 2 * pair + 2], axis=1))
            wide = dot(first[...], jnp.concatenate([high, low], axis=0))
            wide = wide[: 2 * SIDE] + wide[2 * SIDE :]
            for at in range(2):
                re = wide[:SIDE, at * SIDE : (at + 1) * SIDE]
                im = wide[SIDE:, at * SIDE : (at + 1) * SIDE]
                store_halves(
                    turned,
                    2 * pair + at,
                    jnp.concatenate([re * cos + im * sin, im * cos - re * sin], axis=1),
                )

    def load(n, group):
        level = pltpu.roll(levels[...], LANES - channels - WIDE * n, 1) * (1.0 / CODE_TOP)
        at = WIDE * (n - group * slots)
        return [
            signals[group][pl.ds(at + i, SIDE, stride=GROUP_SIZE), :] * level[:, i : i + 1]
            for i in range(WIDE)
        ]

    def second_side(n):
        spectrum = table_right(turned, second)
        of_taps = spectra[WIDE * n // GROUP_SIZE]
        f_re, f_im = of_taps[:, :SIDE], of_taps[:, SIDE:]
        for at in range(WIDE):
            s_re = spectrum[at * SIDE : (at + 1) * SIDE, :SIDE]
            s_im = spectrum[at * SIDE : (at + 1) * SIDE, SIDE:]
            store_halves(
                filtered,
                at,
                jnp.concatenate([s_re * f_re - s_im * f_im, s_re * f_im + s_im * f_re], axis=1),
            )

    def second_side_back():
        back = table_right(filtered, third)
        for at in range(WIDE):
            re = back[at * SIDE : (at + 1) * SIDE, :SIDE]
            im = back[at * SIDE : (at + 1) * SIDE, SIDE:]
            high, low = halves(jnp.concatenate([re * cos - im * sin, im * cos + re * sin], axis=0))
            unturned[: 2 * SIDE, at * SIDE : (at + 1) * SIDE] = high
            unturned[2 * SIDE :, at * SIDE : (at + 1) * SIDE] = low

    def first_side_back(n, group):
        for pair in range(WIDE // 2):
            span = slice(2 * pair * SIDE, (2 * pair + 2) * SIDE)
            done = dot(fourth[...], unturned[: 2 * SIDE, span])
            done = done[:SIDE] + done[SIDE:] + dot(fourth[:SIDE], unturned[2 * SIDE :, span])
            top = jnp.max(jnp.abs(done), axis=0, keepdims=True)
            for i in range(2):
                span = slice(i * SIDE, (i + 1) * SIDE)
                at = WIDE * n + 2 * pair + i
                place = pl.ds(at - group * GROUP_SIZE, SIDE, stride=GROUP_SIZE)
                results[group][place, :] = done[:, span]
                largest[pl.ds(at, 1), :] = top[:, span]

    def scale_group(group):
        span = slice(group * GROUP_SIZE, (group + 1) * GROUP_SIZE)
        scale = code_scale(jnp.max(largest[span, :], axis=1, keepdims=True))
        units[span, :] = jnp.broadcast_to(scale, (GROUP_SIZE, LANES))

    def pack(slot, group):
        to_units = CODE_TOP / units[group * GROUP_SIZE : (group + 1) * GROUP_SIZE, :]
        for i in range(slot_blocks):
            j = slot * slot_blocks + i
            for a in range(per_block):
                at = a * channels + group * GROUP_SIZE
                place = (j * per_block + a) * GROUP_SIZE
                value = results[group][place : place + GROUP_SIZE, :]
                out_ref[j, at : at + GROUP_SIZE, :] = encode(value, to_units).astype(bf16)

    def step(n, carry):
        first_side_back(n - 3, 0)
        second_side_back()
        second_side(n - 1)
        first_side(load(n, 1))
        return carry

    first_side([taps[pl.ds(g, SIDE, stride=groups), :] for g in range(groups)])
    spectra[...] = table_right(turned, second, groups).reshape(groups, SIDE, 2 * SIDE) * (
        1.0 / (SIDE * SIDE)
    )
    first_side(load(0, 0))
    unpack(0, 1, True)
    second_side(0)
    first_side(load(1, 0))
    unpack(1, 1, True)
    second_side_back()
    second_side(1)
    first_side(load(2, 0))
    unpack(2, 1, True)
    first_side_back(0, 0)
    second_side_back()
    second_side(2)
    first_side(load(3, 0))
    unpack(3, 1, True)
    lax.fori_loop(4, 7, step, 0)
    scale_group(0)
    pack(0, 0)
    first_side_back(4, 1)
    second_side_back()
    second_side(6)
    first_side(load(7, 1))
    pack(1, 0)
    first_side_back(5, 1)
    second_side_back()
    second_side(7)
    pack(2, 0)
    first_side_back(6, 1)
    second_side_back()
    pack(3, 0)
    first_side_back(7, 1)
    scale_group(1)

    diagonal = lax.broadcasted_iota(jnp.int32, (channels, LANES), 1) == lax.broadcasted_iota(
        jnp.int32, (channels, LANES), 0
    )
    scale_row = jnp.sum(jnp.where(diagonal, units[...], 0.0), axis=0, keepdims=True)
    back_tails[pl.ds(0, blocks, stride=8), :] = jnp.broadcast_to(scale_row, (blocks, LANES))
    back_tails[pl.ds(7, blocks, stride=8), :] = jnp.zeros((blocks, LANES), f32)
    out_ref[:, data : data + 8, :] = back_tails[...].reshape(blocks, 8, LANES).astype(bf16)
    for slot in range(slots):
        pack(slot, 1)
        out_copy(slot).start()
    for slot in range(slots):
        out_copy(slot).wait()


def local_kernel(q_ref, k_ref, v_ref, w_ref, skip_ref, q_out, s_out, ends_out, pads):
    rows, channels = q_ref.shape

    def column(block, carry):
        lanes = pl.ds(pl.multiple_of(block * LANES, LANES), LANES)
        for step in range(rows // SIDE):
            shorts = []
            for at, ref in enumerate((q_ref, k_ref, v_ref)):
                if step == 0:
                    before = jnp.zeros((8, LANES), f32)
                else:
                    before = ref[step * SIDE - 16 : step * SIDE, lanes].astype(f32)[8:]
                shorts.append(
                    short_conv(ref, step * SIDE, lanes, before, w_ref[at, :, lanes], pads.at[at])
                )
            if step == 0:
                ends_out[0:2, lanes] = shorts[1][0:2]
                ends_out[2:4, lanes] = shorts[2][0:2]
            span = slice(step * SIDE, (step + 1) * SIDE)
            q_out[span, lanes] = shorts[0]
            s_out[span, lanes] = skip_ref[:, lanes] * (shorts[1] * shorts[2])
        return carry

    ends_out[...] = jnp.zeros_like(ends_out)
    lax.fori_loop(0, channels // LANES, column, 0)


def join_kernel(
    in_ref, q_ref, s_ref, ends_ref, w_ref, skip_ref, out_hbm, out_buf, units, fixes, sems
):
    rows, channels = q_ref.shape
    blocks = channels // LANES
    sources = in_ref.shape[0] // blocks
    per = LANES // sources
    steps = rows // SIDE
    base = steps * per
    lane = lax.broadcasted_iota(jnp.int32, (8, LANES), 1)
    for block in range(blocks):
        lanes = slice(block * LANES, (block + 1) * LANES)
        tail = jnp.zeros((8, LANES), f32)
        for i in range(sources):
            part = in_ref[block * sources + i, base : base + 8, :].astype(f32)
            tail = jnp.where(lane // per == i, pltpu.roll(part, i * per, 1), tail)
        units[:, lanes] = tail[0:1] * (1.0 / CODE_TOP)
        adds = []
        for at in range(3):
            ago_2, ago_1 = tail[1 + 2 * at : 2 + 2 * at], tail[2 + 2 * at : 3 + 2 * at]
            weight_1, weight_2 = w_ref[at, 1:2, lanes], w_ref[at, 2:3, lanes]
            adds.append((weight_1 * ago_1 + weight_2 * ago_2, weight_2 * ago_1))
        for token in range(2):
            k_short = ends_ref[token : token + 1, lanes] + adds[1][token]
            v_short = ends_ref[2 + token : 3 + token, lanes] + adds[2][token]
            fixes[token : token + 1, lanes] = q_ref[token : token + 1, lanes] + adds[0][token]
            fixes[2 + token : 3 + token, lanes] = skip_ref[:, lanes] * (k_short * v_short)

    first_rows = lax.broadcasted_iota(jnp.int32, (8, LANES), 0) < 2
    copies = []
    for step in range(steps):
        span = slice(step * SIDE, (step + 1) * SIDE)

        def column(block, carry, step=step, span=span):
            lanes = pl.ds(pl.multiple_of(block * LANES, LANES), LANES)
            first = pl.multiple_of(block * sources, sources)
            code = in_ref[pl.ds(first, sources), step * per : (step + 1) * per, :]
            tile = code.astype(f32).reshape(LANES, SIDE).T
            long_conv = decode(tile, units[:, lanes])
            q_short, skipped = q_ref[span, lanes], s_ref[span, lanes]
            if step == 0:
                fix = fixes[:, lanes]
                q_start = jnp.where(first_rows, fix, q_short[:8])
                s_start = jnp.where(first_rows, pltpu.roll(fix, 6, 0), skipped[:8])
                q_short = jnp.concatenate([q_start, q_short[8:]], axis=0)
                skipped = jnp.concatenate([s_start, skipped[8:]], axis=0)
            out_buf[span, lanes] = (q_short * (long_conv + skipped)).astype(bf16)
            return carry

        lax.fori_loop(0, blocks, column, 0, unroll=2)
        rows_at = pl.ds(step * SIDE, SIDE)
        copies.append(
            pltpu.make_async_copy(out_buf.at[rows_at], out_hbm.at[rows_at], sems.at[step])
        )
        copies[-1].start()
    for copy in copies:
        copy.wait()


def shards(query_in, key_in, value_in, short_weight, skip_bias, filter_taps):
    rows, channels = query_in.shape
    seq = lax.axis_size("seq")
    own = channels // seq
    blocks = channels // LANES
    groups = own // GROUP_SIZE
    sent = rows * own // LANES
    steps = rows // SIDE
    whole = pl.BlockSpec(memory_space=pltpu.VMEM)
    hbm = pl.BlockSpec(memory_space=pltpu.HBM)
    resident = pltpu.CompilerParams(vmem_limit_bytes=RESIDENT_LIMIT)
    streaming = pltpu.CompilerParams(vmem_limit_bytes=STREAMING_LIMIT)

    message = pl.pallas_call(
        gate_kernel,
        in_specs=[hbm] * 5,
        out_specs=hbm,
        out_shape=jax.ShapeDtypeStruct((seq, sent + 16, LANES), bf16),
        scratch_shapes=[
            pltpu.VMEM((rows, channels), bf16),
            pltpu.VMEM((rows, channels), bf16),
            pltpu.VMEM((16, channels), bf16),
            pltpu.VMEM(short_weight.shape, f32),
            pltpu.VMEM(filter_taps.shape, f32),
            pltpu.VMEM((seq, sent + 16, LANES), bf16),
            pltpu.VMEM((2, 2, 16 + SIDE, LANES), f32),
            pltpu.VMEM((8, channels), f32),
            pltpu.VMEM((2, 8, LANES), f32),
            pltpu.VMEM((2, 8, LANES), f32),
            pltpu.VMEM((2, 2 * steps * filter_taps.shape[0] // blocks, LANES), f32),
            pltpu.SemaphoreType.DMA((4, steps)),
        ],
        compiler_params=streaming,
        name="gate",
    )(query_in, key_in, value_in, short_weight, filter_taps)
    message, query_in, key_in, value_in, short_weight, skip_bias, *known = lax.optimization_barrier(
        (message, query_in, key_in, value_in, short_weight, skip_bias, *tables())
    )
    message = lax.all_to_all(message, "seq", 0, 0)

    q_short, skipped, ends = pl.pallas_call(
        local_kernel,
        in_specs=[whole] * 5,
        out_specs=[whole] * 3,
        out_shape=[
            jax.ShapeDtypeStruct((rows, channels), f32),
            jax.ShapeDtypeStruct((rows, channels), f32),
            jax.ShapeDtypeStruct((8, channels), f32),
        ],
        scratch_shapes=[pltpu.VMEM((3, 16 + SIDE, LANES), f32)],
        compiler_params=resident,
        cost_estimate=pl.CostEstimate(
            flops=20 * rows * channels, bytes_accessed=14 * rows * channels, transcendentals=0
        ),
        name="local",
    )(query_in, key_in, value_in, short_weight, skip_bias[None])
    weights = lax.dynamic_slice_in_dim(short_weight, lax.axis_index("seq") * own, own, axis=2)
    weights = jnp.pad(weights, ((0, 0), (0, 0), (0, LANES - own)))
    message, q_short, skipped, ends, weights = lax.optimization_barrier(
        (message, q_short, skipped, ends, weights)
    )

    table_shapes = [pltpu.VMEM(table.shape, table.dtype) for table in known]
    message = pl.pallas_call(
        mix_kernel,
        in_specs=[hbm] * 7,
        out_specs=hbm,
        out_shape=jax.ShapeDtypeStruct((seq, sent + 8, LANES), bf16),
        scratch_shapes=[
            pltpu.VMEM((seq, sent + 16, LANES), bf16),
            pltpu.VMEM(weights.shape, f32),
            *table_shapes,
            pltpu.VMEM((seq, sent + 8, LANES), bf16),
            *[pltpu.VMEM((seq * sent // groups, LANES), f32)] * (2 * groups),
            pltpu.VMEM((seq * 8, LANES), f32),
            pltpu.VMEM((groups, SIDE, 2 * SIDE), f32),
            pltpu.VMEM((own, LANES), f32),
            pltpu.VMEM((own, LANES), f32),
            pltpu.VMEM((seq * 8, LANES), f32),
            pltpu.VMEM((seq * 8, LANES), f32),
            pltpu.VMEM((SIDE, LANES), f32),
            pltpu.VMEM((seq * own, LANES), f32),
            pltpu.VMEM((WIDE * SIDE, 4 * SIDE), bf16),
            pltpu.VMEM((WIDE * SIDE, 4 * SIDE), bf16),
            pltpu.VMEM((4 * SIDE, WIDE * SIDE), bf16),
            pltpu.SemaphoreType.DMA((own // WIDE // groups,)),
            pltpu.SemaphoreType.DMA((6,)),
            pltpu.SemaphoreType.DMA((own // WIDE // groups,)),
        ],
        compiler_params=streaming,
        name="mix",
    )(message, weights, *known)
    message = lax.all_to_all(message, "seq", 0, 0)

    return pl.pallas_call(
        join_kernel,
        in_specs=[whole] * 6,
        out_specs=hbm,
        out_shape=jax.ShapeDtypeStruct((rows, channels), bf16),
        scratch_shapes=[
            pltpu.VMEM((rows, channels), bf16),
            pltpu.VMEM((1, channels), f32),
            pltpu.VMEM((8, channels), f32),
            pltpu.SemaphoreType.DMA((steps,)),
        ],
        compiler_params=resident,
        name="join",
    )(message, q_short, skipped, ends, short_weight, skip_bias[None])


def solution(mesh):
    in_specs = (
        P("seq", "ch"),
        P("seq", "ch"),
        P("seq", "ch"),
        P(None, None, "ch"),
        P("ch"),
        P("ch", "seq"),
    )
    out_specs = P("seq", "ch")
    return jax.shard_map(shards, mesh=mesh, in_specs=in_specs, out_specs=out_specs, check_vma=False)
```

```python
import math

import jax
import jax.numpy as jnp
import numpy as np
from jax import lax
from jax.experimental import pallas as pl
from jax.experimental.pallas import tpu as pltpu
from jax.sharding import PartitionSpec as P

GROUP_SIZE = 16
SIDE = 128
LANES = 128
LAGS = 6
WIDE = 4
CODE_POWER = 17
CODE_TOP = 2.0 ** (120.0 / CODE_POWER)
CODE_LEAST = 2.0**-126
INV_LN2 = 1.0 / math.log(2.0)
RESIDENT_LIMIT = 12 * 1024 * 1024
STREAMING_LIMIT = 60 * 1024 * 1024

f32, bf16 = jnp.float32, jnp.bfloat16


def encode(value, to_units):
    unit = value * to_units
    square = unit * unit
    fourth = square * square
    eighth = fourth * fourth
    return unit * (eighth * eighth)


def decode(code, from_units):
    size = jnp.maximum(jnp.abs(code), CODE_LEAST)
    root = jnp.exp2(jnp.log(size) * (INV_LN2 * (1.0 / CODE_POWER - 1.0)))
    return code * root * from_units


def code_scale(largest):
    return (jnp.maximum(largest, 1e-30) * 1.01).astype(bf16).astype(f32)


def table_blocks():
    side = np.arange(SIDE)
    inner = 2 * np.pi / SIDE * (side[:, None] * side[None, :] % SIDE)
    outer = 2 * np.pi / (4 * SIDE) * (side[None, :] * (4 * side[:, None] + 1) % (4 * SIDE))
    twist = 2 * np.pi / (4 * SIDE * SIDE) * (side[None, :] * (4 * side[:, None] + 1))
    blocks = []
    for angle in (inner, outer, outer.T, twist):
        for table in (np.cos(angle), np.sin(angle)):
            high = table.astype(jnp.bfloat16)
            blocks += [high, (table - high.astype(np.float64)).astype(jnp.bfloat16)]
    return np.concatenate(blocks, axis=0)


def dot(left, right):
    return jnp.dot(left, right, preferred_element_type=f32)


def halves(value):
    high = value.astype(bf16)
    return high, (value - high.astype(f32)).astype(bf16)


def short_conv(stream, at, lanes, before, weights, padded):
    now = stream[pl.ds(at, SIDE), lanes].astype(f32)
    padded[8:16, :] = before
    padded[16:, :] = now
    return (
        weights[0:1] * now
        + weights[1:2] * padded[15 : 15 + SIDE, :]
        + weights[2:3] * padded[14 : 14 + SIDE, :]
    )


def gate_kernel(
    q_hbm,
    k_hbm,
    v_hbm,
    w_hbm,
    taps_hbm,
    out_hbm,
    k_buf,
    v_buf,
    q_buf,
    w_buf,
    taps_buf,
    out_ref,
    pads,
    scales,
    ends,
    q_ends,
    taps_in,
    sems,
):
    rows, channels = k_buf.shape
    steps = rows // SIDE
    blocks = channels // LANES
    dests = out_ref.shape[0] // blocks
    per = LANES // dests
    base = steps * per
    held = taps_buf.shape[0] // blocks
    groups = held // dests

    def stream_copy(at, step):
        source, target = ((k_hbm, k_buf), (v_hbm, v_buf))[at]
        span = pl.ds(step * SIDE, SIDE)
        return pltpu.make_async_copy(source.at[span], target.at[span], sems.at[at, step])

    def out_copy(step):
        end = base + 16 if step == steps - 1 else (step + 1) * per
        span = pl.ds(step * per, end - step * per)
        return pltpu.make_async_copy(out_ref.at[:, span], out_hbm.at[:, span], sems.at[3, step])

    w_copy = pltpu.make_async_copy(w_hbm, w_buf, sems.at[2, 0])
    taps_copy = pltpu.make_async_copy(taps_hbm, taps_buf, sems.at[2, 1])
    q_copy = pltpu.make_async_copy(q_hbm.at[pl.ds(rows - 16, 16)], q_buf, sems.at[2, 2])
    for step in range(steps):
        for at in range(2):
            stream_copy(at, step).start()
        if step == 0:
            w_copy.start()
    taps_copy.start()
    q_copy.start()
    w_copy.wait()

    for step in range(steps):
        for at in range(2):
            stream_copy(at, step).wait()
        if step == steps - 1:
            taps_copy.wait()
            q_copy.wait()

        def tile(block, step=step):
            lanes = slice(block * LANES, (block + 1) * LANES)
            shorts = []
            for at, buf in enumerate((k_buf, v_buf)):
                if step == 0:
                    before = jnp.zeros((8, LANES), f32)
                else:
                    before = buf[step * SIDE - 16 : step * SIDE, lanes].astype(f32)[8:]
                shorts.append(
                    short_conv(
                        buf, step * SIDE, lanes, before, w_buf[1 + at, :, lanes], pads.at[block, at]
                    )
                )
            gated = shorts[0] * shorts[1]
            scale = code_scale(jnp.max(jnp.abs(gated), axis=0, keepdims=True))
            scales[step : step + 1, lanes] = scale
            code = encode(gated, CODE_TOP / scale).T.astype(bf16)
            span = slice(block * dests, (block + 1) * dests)
            out_ref[span, step * per : (step + 1) * per, :] = code.reshape(dests, per, LANES)

        for block in range(blocks):
            tile(block)
        if step < steps - 1:
            out_copy(step).start()

    def tail(block):
        slot = block
        lanes = slice(block * LANES, (block + 1) * LANES)
        for a in range(steps):
            taps_in[slot, a * held : (a + 1) * held, :] = taps_buf[
                block * held : (block + 1) * held, a * LANES : (a + 1) * LANES
            ]
        taps_at = steps * held
        for a in range(steps):
            for g in range(groups):
                piece = taps_in[slot, pl.ds(a * held + g, dests, stride=groups), :]
                taps_in[slot, pl.ds(taps_at + a * groups + g, dests, stride=8), :] = piece
        own_taps = taps_in[slot, taps_at:, :]
        taps_scale = code_scale(jnp.max(jnp.abs(own_taps), axis=1, keepdims=True))
        taps_code = encode(own_taps, CODE_TOP / taps_scale)
        taps_scale = jnp.broadcast_to(taps_scale, own_taps.shape)
        for at, buf in enumerate((k_buf, v_buf)):
            ends[slot, 4 * at : 4 * at + 2, :] = buf[rows - 16 :, lanes].astype(f32)[14:16]
            ends[slot, 4 * at + 2 : 4 * at + 4, :] = buf[0:16, lanes].astype(f32)[0:2]
        q_ends[slot, 0:2, :] = q_buf[:, lanes].astype(f32)[14:16]
        lane = lax.broadcasted_iota(jnp.int32, (8, LANES), 1)
        for d in range(dests):
            asked = pltpu.roll(q_ends[slot], (LANES + 3 * per - d * per) % LANES, 1)
            kept = pltpu.roll(ends[slot], (LANES - d * per) % LANES, 1)
            scaled = pltpu.roll(scales[:, lanes], (LANES + per - d * per) % LANES, 1)
            of_taps = taps_scale[8 * d : 8 * d + 8]
            last = jnp.where(lane < per, kept, jnp.where(lane < 2 * per, scaled, of_taps))
            last = jnp.where(lane < 3 * per, last, asked)
            both = jnp.concatenate([taps_code[8 * d : 8 * d + 8], last], axis=0).astype(bf16)
            out_ref[block * dests + d, base : base + 16, :] = both

    scales[steps:, :] = jnp.zeros((8 - steps, channels), f32)
    q_ends[...] = jnp.zeros_like(q_ends)
    for block in range(blocks):
        tail(block)
    out_copy(steps - 1).start()
    for step in range(steps):
        out_copy(step).wait()


def mix_kernel(
    in_ref,
    w_ref,
    table_ref,
    out_hbm,
    out_ref,
    signal_0,
    signal_1,
    result_0,
    result_1,
    taps,
    spectra,
    units,
    tails,
    back_tails,
    levels,
    starts,
    turned,
    filtered,
    unturned,
    first_raw,
    third_raw,
    first,
    second,
    third,
    fourth,
    twist,
    out_sems,
):
    signals, results = (signal_0, signal_1), (result_0, result_1)
    groups = len(signals)
    blocks = in_ref.shape[0]
    per_block = SIDE // blocks
    channels = groups * GROUP_SIZE
    data = per_block * channels
    count = channels // WIDE
    slots = count // groups
    slot_blocks = blocks // slots

    def out_copy(slot):
        span = pl.ds(slot * slot_blocks, slot_blocks)
        return pltpu.make_async_copy(out_ref.at[span], out_hbm.at[span], out_sems.at[slot])

    def unpack(slot, group):
        for i in range(slot_blocks):
            j = slot * slot_blocks + i
            for a in range(per_block):
                at = a * channels + group * GROUP_SIZE
                place = (j * per_block + a) * GROUP_SIZE
                code = in_ref[j, at : at + GROUP_SIZE, :].astype(f32)
                signals[group][place : place + GROUP_SIZE, :] = code

    for slot in range(slots):
        unpack(slot, 0)

    def block(at):
        return table_ref[at * SIDE : (at + 1) * SIDE, :]

    for part in range(2):
        inner_cos, inner_sin = block(part), block(2 + part)
        for at in ((0, 2 * SIDE), (4 * SIDE,))[part]:
            second[at : at + SIDE, :SIDE] = inner_cos
            second[at : at + SIDE, SIDE:] = -inner_sin
            second[at + SIDE : at + 2 * SIDE, :SIDE] = inner_sin
            second[at + SIDE : at + 2 * SIDE, SIDE:] = inner_cos
            third[at : at + SIDE, :SIDE] = inner_cos
            third[at : at + SIDE, SIDE:] = inner_sin
            third[at + SIDE : at + 2 * SIDE, :SIDE] = -inner_sin
            third[at + SIDE : at + 2 * SIDE, SIDE:] = inner_cos
        at = 2 * part * SIDE
        for span in (slice(0, SIDE), slice(SIDE, 2 * SIDE)):
            first[at : at + SIDE, span] = block(4 + part)
            first[at + SIDE : at + 2 * SIDE, span] = -block(6 + part)
        fourth[part * SIDE : (part + 1) * SIDE, :SIDE] = block(8 + part)
        fourth[part * SIDE : (part + 1) * SIDE, SIDE:] = -block(10 + part)
        twist[part] = block(12 + 2 * part).astype(f32) + block(13 + 2 * part).astype(f32)

    of_message = in_ref[:, data : data + 16, :].astype(f32)
    tails[...] = of_message[:, 8:].reshape(blocks * 8, LANES)
    taps_code = of_message[:, :8].reshape(blocks * 8, LANES)
    taps[...] = decode(taps_code, 1.0 / CODE_TOP) * tails[:, 2 * channels : 2 * channels + 1]
    for a in range(per_block):
        levels[pl.ds(a, blocks, stride=per_block), :] = tails[pl.ds(a, blocks, stride=8), :]

    def gated_starts():
        block = lax.broadcasted_iota(jnp.int32, (blocks, LANES), 0)
        shorts = []
        for at in range(2):
            ago_2, ago_1, now, later = [
                tails[pl.ds(4 * at + i, blocks, stride=8), :] for i in range(4)
            ]
            ago_2 = jnp.where(block == 0, 0.0, pltpu.roll(ago_2, 1, 0))
            ago_1 = jnp.where(block == 0, 0.0, pltpu.roll(ago_1, 1, 0))
            back_tails[pl.ds(3 + 2 * at, blocks, stride=8), :] = ago_2
            back_tails[pl.ds(4 + 2 * at, blocks, stride=8), :] = ago_1
            taps_0, taps_1, taps_2 = [w_ref[1 + at, i : i + 1, :] for i in range(3)]
            shorts.append(
                (
                    taps_0 * now + taps_1 * ago_1 + taps_2 * ago_2,
                    taps_0 * later + taps_1 * now + taps_2 * ago_1,
                )
            )
        for at in range(2):
            asked = pltpu.roll(tails[pl.ds(at, blocks, stride=8), :], LANES - 3 * channels, 1)
            asked = jnp.where(block == 0, 0.0, pltpu.roll(asked, 1, 0))
            back_tails[pl.ds(1 + at, blocks, stride=8), :] = asked
        packed = [shorts[0][token] * shorts[1][token] for token in range(2)]
        for token in range(2):
            starts[token] = jnp.zeros((SIDE, LANES), f32)
            starts[token, pl.ds(0, blocks, stride=per_block), :] = packed[token]

    gated_starts()

    cos, sin = twist[0], twist[1]

    def store_halves(ref, at, value):
        high, low = halves(value)
        ref[at * SIDE : (at + 1) * SIDE, : 2 * SIDE] = high
        ref[at * SIDE : (at + 1) * SIDE, 2 * SIDE :] = low

    def table_right(ref, table, used=WIDE):
        rows = used * SIDE
        return dot(ref[:rows], table[: 4 * SIDE]) + dot(ref[:rows, : 2 * SIDE], table[4 * SIDE :])

    lane = lax.broadcasted_iota(jnp.int32, (SIDE, LANES), 1)
    starts_block = lax.broadcasted_iota(jnp.int32, (SIDE, LANES), 0) % per_block == 0
    start_masks = [starts_block & (lane == token) for token in range(2)]

    def load(n, group):
        level = pltpu.roll(levels[...], LANES - channels - WIDE * n, 1) * (1.0 / CODE_TOP)
        first_tokens = [pltpu.roll(starts[token], LANES - WIDE * n, 1) for token in range(2)]
        at = WIDE * (n - group * slots)
        values = []
        for i in range(WIDE):
            code = signals[group][pl.ds(at + i, SIDE, stride=GROUP_SIZE), :]
            value = decode(code, level[:, i : i + 1])
            for token in range(2):
                value = jnp.where(start_masks[token], first_tokens[token][:, i : i + 1], value)
            values.append(value)
        return values

    def first_side(values):
        for pair in range(len(values) // 2):
            high, low = halves(jnp.concatenate(values[2 * pair : 2 * pair + 2], axis=1))
            wide = dot(first[...], jnp.concatenate([high, low], axis=0))
            first_raw[pair] = wide[: 2 * SIDE] + wide[2 * SIDE :]

    def turn(used=WIDE):
        for at in range(used):
            span = slice(at % 2 * SIDE, (at % 2 + 1) * SIDE)
            re, im = first_raw[at // 2, :SIDE, span], first_raw[at // 2, SIDE:, span]
            store_halves(
                turned, at, jnp.concatenate([re * cos + im * sin, im * cos - re * sin], axis=1)
            )

    def filter_spectrum(n, spectrum):
        of_taps = spectra[WIDE * n // GROUP_SIZE]
        f_re, f_im = of_taps[:, :SIDE], of_taps[:, SIDE:]
        for at in range(WIDE):
            s_re = spectrum[at * SIDE : (at + 1) * SIDE, :SIDE]
            s_im = spectrum[at * SIDE : (at + 1) * SIDE, SIDE:]
            store_halves(
                filtered,
                at,
                jnp.concatenate([s_re * f_re - s_im * f_im, s_re * f_im + s_im * f_re], axis=1),
            )

    def turn_back():
        for at in range(WIDE):
            re = third_raw[at * SIDE : (at + 1) * SIDE, :SIDE]
            im = third_raw[at * SIDE : (at + 1) * SIDE, SIDE:]
            high, low = halves(jnp.concatenate([re * cos - im * sin, im * cos + re * sin], axis=0))
            unturned[: 2 * SIDE, at * SIDE : (at + 1) * SIDE] = high
            unturned[2 * SIDE :, at * SIDE : (at + 1) * SIDE] = low

    def first_side_back():
        found = []
        for pair in range(WIDE // 2):
            span = slice(2 * pair * SIDE, (2 * pair + 2) * SIDE)
            done = dot(fourth[...], unturned[: 2 * SIDE, span])
            found.append(
                done[:SIDE] + done[SIDE:] + dot(fourth[:SIDE], unturned[2 * SIDE :, span])
            )
        return found

    def finish(n, group, found):
        for i in range(WIDE):
            value = found[i // 2][:, i % 2 * SIDE : (i % 2 + 1) * SIDE]
            top = jnp.max(jnp.max(jnp.abs(value), axis=0, keepdims=True), axis=1, keepdims=True)
            scale = code_scale(top)
            channel = WIDE * n + i
            units[pl.ds(channel, 1), :] = jnp.broadcast_to(scale, (1, LANES))
            place = pl.ds(channel - group * GROUP_SIZE, SIDE, stride=GROUP_SIZE)
            results[group][place, :] = encode(value, CODE_TOP / scale)

    def step(n, load_group, finish_group, active=(True,) * LAGS):
        loads, turns, filters, filtered_back, turns_back, finishes = active
        if filters:
            spectrum = table_right(turned, second)
        if finishes:
            found = first_side_back()
        if turns:
            turn()
        if turns_back:
            turn_back()
        if filtered_back:
            third_raw[...] = table_right(filtered, third)
        if loads:
            first_side(load(n, load_group))
        if finishes:
            finish(n - 5, finish_group, found)
        if filters:
            filter_spectrum(n - 2, spectrum)

    def pack(slot, group):
        for i in range(slot_blocks):
            j = slot * slot_blocks + i
            for a in range(per_block):
                at = a * channels + group * GROUP_SIZE
                place = (j * per_block + a) * GROUP_SIZE
                code = results[group][place : place + GROUP_SIZE, :]
                out_ref[j, at : at + GROUP_SIZE, :] = code.astype(bf16)

    first_side([taps[pl.ds(g, SIDE, stride=groups), :] for g in range(groups)])
    turn(groups)
    spectra[...] = table_right(turned, second, groups).reshape(groups, SIDE, 2 * SIDE) * (
        1.0 / (SIDE * SIDE)
    )
    for n in range(slots):
        step(n, 0, 0, tuple(n >= lag for lag in range(LAGS)))
        unpack(n, 1)
    step(slots, 1, 0, tuple(slots >= lag for lag in range(LAGS)))

    def steady(n, carry):
        step(n, 1, 0)
        return carry

    lax.fori_loop(slots + 1, count, steady, 0)
    for n in range(count, count + LAGS - 1):
        step(n, 1, int(n - LAGS + 1 >= slots), tuple(n - lag < count for lag in range(LAGS)))
        if n > count:
            pack(n - count - 1, 0)

    diagonal = lax.broadcasted_iota(jnp.int32, (channels, LANES), 1) == lax.broadcasted_iota(
        jnp.int32, (channels, LANES), 0
    )
    scale_row = jnp.sum(jnp.where(diagonal, units[...], 0.0), axis=0, keepdims=True)
    back_tails[pl.ds(0, blocks, stride=8), :] = jnp.broadcast_to(scale_row, (blocks, LANES))
    back_tails[pl.ds(7, blocks, stride=8), :] = jnp.zeros((blocks, LANES), f32)
    out_ref[:, data : data + 8, :] = back_tails[...].reshape(blocks, 8, LANES).astype(bf16)
    for slot in range(slots):
        pack(slot, 1)
        out_copy(slot).start()
    for slot in range(slots):
        out_copy(slot).wait()


def local_kernel(q_ref, k_ref, v_ref, w_ref, skip_ref, q_out, s_out, ends_out, pads):
    rows, channels = q_ref.shape

    def column(block, carry):
        lanes = pl.ds(pl.multiple_of(block * LANES, LANES), LANES)
        for step in range(rows // SIDE):
            shorts = []
            for at, ref in enumerate((q_ref, k_ref, v_ref)):
                if step == 0:
                    before = jnp.zeros((8, LANES), f32)
                else:
                    before = ref[step * SIDE - 16 : step * SIDE, lanes].astype(f32)[8:]
                shorts.append(
                    short_conv(ref, step * SIDE, lanes, before, w_ref[at, :, lanes], pads.at[at])
                )
            if step == 0:
                ends_out[0:2, lanes] = shorts[1][0:2]
                ends_out[2:4, lanes] = shorts[2][0:2]
            span = slice(step * SIDE, (step + 1) * SIDE)
            q_out[span, lanes] = shorts[0]
            s_out[span, lanes] = skip_ref[:, lanes] * (shorts[1] * shorts[2])
        return carry

    ends_out[...] = jnp.zeros_like(ends_out)
    lax.fori_loop(0, channels // LANES, column, 0)


def join_kernel(
    in_ref, q_ref, s_ref, ends_ref, w_ref, skip_ref, out_hbm, out_buf, units, fixes, sems
):
    rows, channels = q_ref.shape
    blocks = channels // LANES
    sources = in_ref.shape[0] // blocks
    per = LANES // sources
    steps = rows // SIDE
    base = steps * per
    lane = lax.broadcasted_iota(jnp.int32, (8, LANES), 1)
    for block in range(blocks):
        lanes = slice(block * LANES, (block + 1) * LANES)
        tail = jnp.zeros((8, LANES), f32)
        for i in range(sources):
            part = in_ref[block * sources + i, base : base + 8, :].astype(f32)
            tail = jnp.where(lane // per == i, pltpu.roll(part, i * per, 1), tail)
        units[:, lanes] = tail[0:1] * (1.0 / CODE_TOP)
        adds = []
        for at in range(3):
            ago_2, ago_1 = tail[1 + 2 * at : 2 + 2 * at], tail[2 + 2 * at : 3 + 2 * at]
            weight_1, weight_2 = w_ref[at, 1:2, lanes], w_ref[at, 2:3, lanes]
            adds.append((weight_1 * ago_1 + weight_2 * ago_2, weight_2 * ago_1))
        for token in range(2):
            k_short = ends_ref[token : token + 1, lanes] + adds[1][token]
            v_short = ends_ref[2 + token : 3 + token, lanes] + adds[2][token]
            fixes[token : token + 1, lanes] = q_ref[token : token + 1, lanes] + adds[0][token]
            fixes[2 + token : 3 + token, lanes] = skip_ref[:, lanes] * (k_short * v_short)

    first_rows = lax.broadcasted_iota(jnp.int32, (8, LANES), 0) < 2
    copies = []
    for step in range(steps):
        span = slice(step * SIDE, (step + 1) * SIDE)

        for block in range(blocks):
            lanes = slice(block * LANES, (block + 1) * LANES)
            of_block = slice(block * sources, (block + 1) * sources)
            code = in_ref[of_block, step * per : (step + 1) * per, :]
            tile = code.astype(f32).reshape(LANES, SIDE).T
            long_conv = decode(tile, units[:, lanes])
            q_short, skipped = q_ref[span, lanes], s_ref[span, lanes]
            if step == 0:
                fix = fixes[:, lanes]
                q_start = jnp.where(first_rows, fix, q_short[:8])
                s_start = jnp.where(first_rows, pltpu.roll(fix, 6, 0), skipped[:8])
                q_short = jnp.concatenate([q_start, q_short[8:]], axis=0)
                skipped = jnp.concatenate([s_start, skipped[8:]], axis=0)
            out_buf[span, lanes] = (q_short * (long_conv + skipped)).astype(bf16)
        rows_at = pl.ds(step * SIDE, SIDE)
        copies.append(
            pltpu.make_async_copy(out_buf.at[rows_at], out_hbm.at[rows_at], sems.at[step])
        )
        copies[-1].start()
    for copy in copies:
        copy.wait()


def shards(query_in, key_in, value_in, short_weight, skip_bias, filter_taps):
    rows, channels = query_in.shape
    seq = lax.axis_size("seq")
    own = channels // seq
    blocks = channels // LANES
    groups = own // GROUP_SIZE
    sent = rows * own // LANES
    steps = rows // SIDE
    whole = pl.BlockSpec(memory_space=pltpu.VMEM)
    hbm = pl.BlockSpec(memory_space=pltpu.HBM)
    resident = pltpu.CompilerParams(vmem_limit_bytes=RESIDENT_LIMIT)
    streaming = pltpu.CompilerParams(vmem_limit_bytes=STREAMING_LIMIT)

    message = pl.pallas_call(
        gate_kernel,
        in_specs=[hbm] * 5,
        out_specs=hbm,
        out_shape=jax.ShapeDtypeStruct((seq, sent + 16, LANES), bf16),
        scratch_shapes=[
            pltpu.VMEM((rows, channels), bf16),
            pltpu.VMEM((rows, channels), bf16),
            pltpu.VMEM((16, channels), bf16),
            pltpu.VMEM(short_weight.shape, f32),
            pltpu.VMEM(filter_taps.shape, f32),
            pltpu.VMEM((seq, sent + 16, LANES), bf16),
            pltpu.VMEM((blocks, 2, 16 + SIDE, LANES), f32),
            pltpu.VMEM((8, channels), f32),
            pltpu.VMEM((blocks, 8, LANES), f32),
            pltpu.VMEM((blocks, 8, LANES), f32),
            pltpu.VMEM((blocks, 2 * steps * filter_taps.shape[0] // blocks, LANES), f32),
            pltpu.SemaphoreType.DMA((4, steps)),
        ],
        compiler_params=streaming,
        name="gate",
    )(query_in, key_in, value_in, short_weight, filter_taps)
    message, query_in, key_in, value_in, short_weight, skip_bias, known = lax.optimization_barrier(
        (message, query_in, key_in, value_in, short_weight, skip_bias, table_blocks())
    )
    message = lax.all_to_all(message, "seq", 0, 0)

    q_short, skipped, ends = pl.pallas_call(
        local_kernel,
        in_specs=[whole] * 5,
        out_specs=[whole] * 3,
        out_shape=[
            jax.ShapeDtypeStruct((rows, channels), f32),
            jax.ShapeDtypeStruct((rows, channels), f32),
            jax.ShapeDtypeStruct((8, channels), f32),
        ],
        scratch_shapes=[pltpu.VMEM((3, 16 + SIDE, LANES), f32)],
        compiler_params=resident,
        cost_estimate=pl.CostEstimate(
            flops=20 * rows * channels, bytes_accessed=14 * rows * channels, transcendentals=0
        ),
        name="local",
    )(query_in, key_in, value_in, short_weight, skip_bias[None])
    weights = lax.dynamic_slice_in_dim(short_weight, lax.axis_index("seq") * own, own, axis=2)
    weights = jnp.pad(weights, ((0, 0), (0, 0), (0, LANES - own)))
    message, q_short, skipped, ends, weights = lax.optimization_barrier(
        (message, q_short, skipped, ends, weights)
    )

    message = pl.pallas_call(
        mix_kernel,
        in_specs=[whole] * 3,
        out_specs=hbm,
        out_shape=jax.ShapeDtypeStruct((seq, sent + 8, LANES), bf16),
        scratch_shapes=[
            pltpu.VMEM((seq, sent + 8, LANES), bf16),
            *[pltpu.VMEM((seq * sent // groups, LANES), f32)] * (2 * groups),
            pltpu.VMEM((seq * 8, LANES), f32),
            pltpu.VMEM((groups, SIDE, 2 * SIDE), f32),
            pltpu.VMEM((own, LANES), f32),
            pltpu.VMEM((seq * 8, LANES), f32),
            pltpu.VMEM((seq * 8, LANES), f32),
            pltpu.VMEM((SIDE, LANES), f32),
            pltpu.VMEM((2, SIDE, LANES), f32),
            pltpu.VMEM((WIDE * SIDE, 4 * SIDE), bf16),
            pltpu.VMEM((WIDE * SIDE, 4 * SIDE), bf16),
            pltpu.VMEM((4 * SIDE, WIDE * SIDE), bf16),
            pltpu.VMEM((WIDE // 2, 2 * SIDE, 2 * SIDE), f32),
            pltpu.VMEM((WIDE * SIDE, 2 * SIDE), f32),
            pltpu.VMEM((4 * SIDE, 2 * SIDE), bf16),
            pltpu.VMEM((6 * SIDE, 2 * SIDE), bf16),
            pltpu.VMEM((6 * SIDE, 2 * SIDE), bf16),
            pltpu.VMEM((2 * SIDE, 2 * SIDE), bf16),
            pltpu.VMEM((2, SIDE, LANES), f32),
            pltpu.SemaphoreType.DMA((own // WIDE // groups,)),
        ],
        compiler_params=resident,
        name="mix",
    )(message, weights, known)
    message = lax.all_to_all(message, "seq", 0, 0)

    return pl.pallas_call(
        join_kernel,
        in_specs=[whole] * 6,
        out_specs=hbm,
        out_shape=jax.ShapeDtypeStruct((rows, channels), bf16),
        scratch_shapes=[
            pltpu.VMEM((rows, channels), bf16),
            pltpu.VMEM((1, channels), f32),
            pltpu.VMEM((8, channels), f32),
            pltpu.SemaphoreType.DMA((steps,)),
        ],
        compiler_params=resident,
        name="join",
    )(message, q_short, skipped, ends, short_weight, skip_bias[None])


def solution(mesh):
    in_specs = (
        P("seq", "ch"),
        P("seq", "ch"),
        P("seq", "ch"),
        P(None, None, "ch"),
        P("ch"),
        P("ch", "seq"),
    )
    out_specs = P("seq", "ch")
    return jax.shard_map(shards, mesh=mesh, in_specs=in_specs, out_specs=out_specs, check_vma=False)
```

```python
import math

import jax
import jax.numpy as jnp
import numpy as np
from jax import lax
from jax.experimental import pallas as pl
from jax.experimental.pallas import tpu as pltpu
from jax.sharding import PartitionSpec as P

GROUP_SIZE = 16
SIDE = 128
LANES = 128
LAGS = 7
WIDE = 4
CODE_POWER = 17
CODE_TOP = 2.0 ** (120.0 / CODE_POWER)
CODE_LEAST = 2.0**-126
INV_LN2 = 1.0 / math.log(2.0)
RESIDENT_LIMIT = 12 * 1024 * 1024
MIX_LIMIT = 20 * 1024 * 1024
STREAMING_LIMIT = 60 * 1024 * 1024

f32, bf16 = jnp.float32, jnp.bfloat16


def encode(value, to_units):
    unit = value * to_units
    square = unit * unit
    fourth = square * square
    eighth = fourth * fourth
    return unit * (eighth * eighth)


def decode(code, from_units):
    size = jnp.maximum(jnp.abs(code), CODE_LEAST)
    root = jnp.exp2(jnp.log(size) * (INV_LN2 * (1.0 / CODE_POWER - 1.0)))
    return code * root * from_units


def code_scale(largest):
    return (jnp.maximum(largest, 1e-30) * 1.01).astype(bf16).astype(f32)


def table_blocks():
    side = np.arange(SIDE)
    inner = 2 * np.pi / SIDE * (side[:, None] * side[None, :] % SIDE)
    outer = 2 * np.pi / (4 * SIDE) * (side[None, :] * (4 * side[:, None] + 1) % (4 * SIDE))
    twist = 2 * np.pi / (4 * SIDE * SIDE) * (side[None, :] * (4 * side[:, None] + 1))
    blocks = []
    for angle in (inner, outer, outer.T, twist):
        for table in (np.cos(angle), np.sin(angle)):
            high = table.astype(jnp.bfloat16)
            blocks += [high, (table - high.astype(np.float64)).astype(jnp.bfloat16)]
    return np.concatenate(blocks, axis=0)


def dot(left, right):
    return jnp.dot(left, right, preferred_element_type=f32)


def halves(value):
    high = value.astype(bf16)
    return high, (value - high.astype(f32)).astype(bf16)


def short_conv(stream, at, lanes, before, weights, padded):
    now = stream[pl.ds(at, SIDE), lanes].astype(f32)
    padded[8:16, :] = before
    padded[16:, :] = now
    return (
        weights[0:1] * now
        + weights[1:2] * padded[15 : 15 + SIDE, :]
        + weights[2:3] * padded[14 : 14 + SIDE, :]
    )


def gate_kernel(
    q_hbm,
    k_hbm,
    v_hbm,
    w_hbm,
    taps_hbm,
    out_hbm,
    k_buf,
    v_buf,
    q_buf,
    w_buf,
    taps_buf,
    out_ref,
    pads,
    scales,
    ends,
    q_ends,
    taps_in,
    sems,
    last_sems,
):
    rows, channels = k_buf.shape
    steps = rows // SIDE
    blocks = channels // LANES
    dests = out_ref.shape[0] // blocks
    per = LANES // dests
    base = steps * per
    held = taps_buf.shape[0] // blocks
    groups = held // dests

    def stream_copy(at, step):
        source, target = ((k_hbm, k_buf), (v_hbm, v_buf))[at]
        span = pl.ds(step * SIDE, SIDE)
        return pltpu.make_async_copy(source.at[span], target.at[span], sems.at[at, step])

    def out_copy(step):
        span = pl.ds(step * per, per)
        return pltpu.make_async_copy(out_ref.at[:, span], out_hbm.at[:, span], sems.at[3, step])

    def last_copy(block):
        dest, span = pl.ds(block * dests, dests), pl.ds(base - per, per + 16)
        return pltpu.make_async_copy(
            out_ref.at[dest, span], out_hbm.at[dest, span], last_sems.at[block]
        )

    w_copy = pltpu.make_async_copy(w_hbm, w_buf, sems.at[2, 0])
    taps_copy = pltpu.make_async_copy(taps_hbm, taps_buf, sems.at[2, 1])
    q_copy = pltpu.make_async_copy(q_hbm.at[pl.ds(rows - 16, 16)], q_buf, sems.at[2, 2])
    for step in range(steps):
        for at in range(2):
            stream_copy(at, step).start()
        if step == 0:
            w_copy.start()
    taps_copy.start()
    q_copy.start()
    w_copy.wait()

    for step in range(steps):
        for at in range(2):
            stream_copy(at, step).wait()
        if step == steps - 1:
            taps_copy.wait()
            q_copy.wait()

        def tile(block, step=step):
            lanes = slice(block * LANES, (block + 1) * LANES)
            shorts = []
            for at, buf in enumerate((k_buf, v_buf)):
                if step == 0:
                    before = jnp.zeros((8, LANES), f32)
                else:
                    before = buf[step * SIDE - 16 : step * SIDE, lanes].astype(f32)[8:]
                shorts.append(
                    short_conv(
                        buf, step * SIDE, lanes, before, w_buf[1 + at, :, lanes], pads.at[block, at]
                    )
                )
            gated = shorts[0] * shorts[1]
            scale = code_scale(jnp.max(jnp.abs(gated), axis=0, keepdims=True))
            scales[step : step + 1, lanes] = scale
            code = encode(gated, CODE_TOP / scale).T.astype(bf16)
            span = slice(block * dests, (block + 1) * dests)
            out_ref[span, step * per : (step + 1) * per, :] = code.reshape(dests, per, LANES)

        if step < steps - 1:
            for block in range(blocks):
                tile(block)
            out_copy(step).start()

    def tail(block):
        slot = block
        lanes = slice(block * LANES, (block + 1) * LANES)
        for a in range(steps):
            taps_in[slot, a * held : (a + 1) * held, :] = taps_buf[
                block * held : (block + 1) * held, a * LANES : (a + 1) * LANES
            ]
        taps_at = steps * held
        for a in range(steps):
            for g in range(groups):
                piece = taps_in[slot, pl.ds(a * held + g, dests, stride=groups), :]
                taps_in[slot, pl.ds(taps_at + a * groups + g, dests, stride=8), :] = piece
        own_taps = taps_in[slot, taps_at:, :]
        taps_scale = code_scale(jnp.max(jnp.abs(own_taps), axis=1, keepdims=True))
        taps_code = encode(own_taps, CODE_TOP / taps_scale)
        taps_scale = jnp.broadcast_to(taps_scale, own_taps.shape)
        for at, buf in enumerate((k_buf, v_buf)):
            ends[slot, 4 * at : 4 * at + 2, :] = buf[rows - 16 :, lanes].astype(f32)[14:16]
            ends[slot, 4 * at + 2 : 4 * at + 4, :] = buf[0:16, lanes].astype(f32)[0:2]
        q_ends[slot, 0:2, :] = q_buf[:, lanes].astype(f32)[14:16]
        lane = lax.broadcasted_iota(jnp.int32, (8, LANES), 1)
        for d in range(dests):
            asked = pltpu.roll(q_ends[slot], (LANES + 3 * per - d * per) % LANES, 1)
            kept = pltpu.roll(ends[slot], (LANES - d * per) % LANES, 1)
            scaled = pltpu.roll(scales[:, lanes], (LANES + per - d * per) % LANES, 1)
            of_taps = taps_scale[8 * d : 8 * d + 8]
            last = jnp.where(lane < per, kept, jnp.where(lane < 2 * per, scaled, of_taps))
            last = jnp.where(lane < 3 * per, last, asked)
            both = jnp.concatenate([taps_code[8 * d : 8 * d + 8], last], axis=0).astype(bf16)
            out_ref[block * dests + d, base : base + 16, :] = both

    scales[steps:, :] = jnp.zeros((8 - steps, channels), f32)
    q_ends[...] = jnp.zeros_like(q_ends)
    for block in range(blocks):
        tile(block)
        tail(block)
        if block % 2 == 1:
            last_copy(block - 1).start()
            last_copy(block).start()
    for step in range(steps - 1):
        out_copy(step).wait()
    for block in range(blocks):
        last_copy(block).wait()


def mix_kernel(
    in_ref,
    w_ref,
    table_ref,
    out_hbm,
    out_ref,
    signal_0,
    signal_1,
    result_0,
    result_1,
    taps,
    spectra,
    units,
    tails,
    back_tails,
    levels,
    starts,
    turned,
    filtered,
    unturned,
    first_raw,
    third_raw,
    fourth_raw,
    first,
    second,
    third,
    fourth,
    twist,
    out_sems,
):
    signals, results = (signal_0, signal_1), (result_0, result_1)
    groups = len(signals)
    blocks = in_ref.shape[0]
    per_block = SIDE // blocks
    channels = groups * GROUP_SIZE
    data = per_block * channels
    count = channels // WIDE
    slots = count // groups
    slot_blocks = blocks // slots

    def out_copy(slot):
        span = pl.ds(slot * slot_blocks, slot_blocks)
        return pltpu.make_async_copy(out_ref.at[span], out_hbm.at[span], out_sems.at[slot])

    def unpack(slot, group):
        for i in range(slot_blocks):
            j = slot * slot_blocks + i
            for a in range(per_block):
                at = a * channels + group * GROUP_SIZE
                place = (j * per_block + a) * GROUP_SIZE
                code = in_ref[j, at : at + GROUP_SIZE, :].astype(f32)
                signals[group][place : place + GROUP_SIZE, :] = code

    for slot in range(slots):
        unpack(slot, 0)

    def block(at):
        return table_ref[at * SIDE : (at + 1) * SIDE, :]

    for part in range(2):
        inner_cos, inner_sin = block(part), block(2 + part)
        for at in ((0, 2 * SIDE), (4 * SIDE,))[part]:
            second[at : at + SIDE, :SIDE] = inner_cos
            second[at : at + SIDE, SIDE:] = -inner_sin
            second[at + SIDE : at + 2 * SIDE, :SIDE] = inner_sin
            second[at + SIDE : at + 2 * SIDE, SIDE:] = inner_cos
            third[at : at + SIDE, :SIDE] = inner_cos
            third[at : at + SIDE, SIDE:] = inner_sin
            third[at + SIDE : at + 2 * SIDE, :SIDE] = -inner_sin
            third[at + SIDE : at + 2 * SIDE, SIDE:] = inner_cos
        at = 2 * part * SIDE
        for span in (slice(0, SIDE), slice(SIDE, 2 * SIDE)):
            first[at : at + SIDE, span] = block(4 + part)
            first[at + SIDE : at + 2 * SIDE, span] = -block(6 + part)
        fourth[part * SIDE : (part + 1) * SIDE, :SIDE] = block(8 + part)
        fourth[part * SIDE : (part + 1) * SIDE, SIDE:] = -block(10 + part)
        twist[part] = block(12 + 2 * part).astype(f32) + block(13 + 2 * part).astype(f32)

    of_message = in_ref[:, data : data + 16, :].astype(f32)
    tails[...] = of_message[:, 8:].reshape(blocks * 8, LANES)
    taps_code = of_message[:, :8].reshape(blocks * 8, LANES)
    taps[...] = decode(taps_code, 1.0 / CODE_TOP) * tails[:, 2 * channels : 2 * channels + 1]
    for a in range(per_block):
        levels[pl.ds(a, blocks, stride=per_block), :] = tails[pl.ds(a, blocks, stride=8), :]

    def gated_starts():
        block = lax.broadcasted_iota(jnp.int32, (blocks, LANES), 0)
        shorts = []
        for at in range(2):
            ago_2, ago_1, now, later = [
                tails[pl.ds(4 * at + i, blocks, stride=8), :] for i in range(4)
            ]
            ago_2 = jnp.where(block == 0, 0.0, pltpu.roll(ago_2, 1, 0))
            ago_1 = jnp.where(block == 0, 0.0, pltpu.roll(ago_1, 1, 0))
            back_tails[pl.ds(3 + 2 * at, blocks, stride=8), :] = ago_2
            back_tails[pl.ds(4 + 2 * at, blocks, stride=8), :] = ago_1
            taps_0, taps_1, taps_2 = [w_ref[1 + at, i : i + 1, :] for i in range(3)]
            shorts.append(
                (
                    taps_0 * now + taps_1 * ago_1 + taps_2 * ago_2,
                    taps_0 * later + taps_1 * now + taps_2 * ago_1,
                )
            )
        for at in range(2):
            asked = pltpu.roll(tails[pl.ds(at, blocks, stride=8), :], LANES - 3 * channels, 1)
            asked = jnp.where(block == 0, 0.0, pltpu.roll(asked, 1, 0))
            back_tails[pl.ds(1 + at, blocks, stride=8), :] = asked
        from_lane = lax.broadcasted_iota(jnp.int32, (LANES, LANES), 0)
        to_lane = lax.broadcasted_iota(jnp.int32, (LANES, LANES), 1)
        known = lax.broadcasted_iota(jnp.int32, (blocks, LANES), 1) < channels
        spread = jnp.zeros((blocks, LANES), f32)
        for token in range(2):
            gated = jnp.where(known, shorts[0][token] * shorts[1][token], 0.0)
            place = jnp.where(to_lane == 2 * from_lane + token, 1.0, 0.0).astype(bf16)
            for part in halves(gated):
                spread = spread + dot(part, place)
        starts[...] = jnp.zeros((SIDE, LANES), f32)
        starts[pl.ds(0, blocks, stride=per_block), :] = spread

    gated_starts()

    cos, sin = twist[0], twist[1]

    def store_halves(ref, at, value):
        high, low = halves(value)
        ref[at * SIDE : (at + 1) * SIDE, : 2 * SIDE] = high
        ref[at * SIDE : (at + 1) * SIDE, 2 * SIDE :] = low

    def table_right(ref, table, used=WIDE):
        rows = used * SIDE
        return dot(ref[:rows], table[: 4 * SIDE]) + dot(ref[:rows, : 2 * SIDE], table[4 * SIDE :])

    lane = lax.broadcasted_iota(jnp.int32, (SIDE, LANES), 1)
    is_start = (lax.broadcasted_iota(jnp.int32, (SIDE, LANES), 0) % per_block == 0) & (lane < 2)

    def load(n, group):
        level = pltpu.roll(levels[...], LANES - channels - WIDE * n, 1) * (1.0 / CODE_TOP)
        at = WIDE * (n - group * slots)
        values = []
        for i in range(WIDE):
            code = signals[group][pl.ds(at + i, SIDE, stride=GROUP_SIZE), :]
            value = decode(code, level[:, i : i + 1])
            start = pltpu.roll(starts[...], (LANES - 2 * (WIDE * n + i)) % LANES, 1)
            values.append(jnp.where(is_start, start, value))
        return values

    def first_side(values):
        for pair in range(len(values) // 2):
            high, low = halves(jnp.concatenate(values[2 * pair : 2 * pair + 2], axis=1))
            wide = dot(first[...], jnp.concatenate([high, low], axis=0))
            first_raw[pair] = wide[: 2 * SIDE] + wide[2 * SIDE :]

    def turn(used=WIDE):
        for at in range(used):
            span = slice(at % 2 * SIDE, (at % 2 + 1) * SIDE)
            re, im = first_raw[at // 2, :SIDE, span], first_raw[at // 2, SIDE:, span]
            store_halves(
                turned, at, jnp.concatenate([re * cos + im * sin, im * cos - re * sin], axis=1)
            )

    def filter_spectrum(n, spectrum):
        of_taps = spectra[WIDE * n // GROUP_SIZE]
        f_re, f_im = of_taps[:, :SIDE], of_taps[:, SIDE:]
        for at in range(WIDE):
            s_re = spectrum[at * SIDE : (at + 1) * SIDE, :SIDE]
            s_im = spectrum[at * SIDE : (at + 1) * SIDE, SIDE:]
            store_halves(
                filtered,
                at,
                jnp.concatenate([s_re * f_re - s_im * f_im, s_re * f_im + s_im * f_re], axis=1),
            )

    def turn_back():
        for at in range(WIDE):
            re = third_raw[at * SIDE : (at + 1) * SIDE, :SIDE]
            im = third_raw[at * SIDE : (at + 1) * SIDE, SIDE:]
            high, low = halves(jnp.concatenate([re * cos - im * sin, im * cos + re * sin], axis=0))
            unturned[: 2 * SIDE, at * SIDE : (at + 1) * SIDE] = high
            unturned[2 * SIDE :, at * SIDE : (at + 1) * SIDE] = low

    def first_side_back():
        for pair in range(WIDE // 2):
            span = slice(2 * pair * SIDE, (2 * pair + 2) * SIDE)
            done = dot(fourth[...], unturned[: 2 * SIDE, span])
            fourth_raw[pair] = (
                done[:SIDE] + done[SIDE:] + dot(fourth[:SIDE], unturned[2 * SIDE :, span])
            )

    def finish(n, group):
        for i in range(WIDE):
            value = fourth_raw[i // 2, :, i % 2 * SIDE : (i % 2 + 1) * SIDE]
            top = jnp.max(jnp.max(jnp.abs(value), axis=0, keepdims=True), axis=1, keepdims=True)
            scale = code_scale(top)
            channel = WIDE * n + i
            units[pl.ds(channel, 1), :] = jnp.broadcast_to(scale, (1, LANES))
            place = pl.ds(channel - group * GROUP_SIZE, SIDE, stride=GROUP_SIZE)
            results[group][place, :] = encode(value, CODE_TOP / scale)

    def step(n, load_group, finish_group, active=(True,) * LAGS):
        loads, turns, filters, filtered_back, turns_back, sides_back, finishes = active
        if finishes:
            finish(n - 6, finish_group)
        if filters:
            spectrum = table_right(turned, second)
        if sides_back:
            first_side_back()
        if turns:
            turn()
        if turns_back:
            turn_back()
        if filtered_back:
            third_raw[...] = table_right(filtered, third)
        if loads:
            first_side(load(n, load_group))
        if filters:
            filter_spectrum(n - 2, spectrum)

    def pack(slot, half):
        group, above = half // 2, half % 2 * 8
        for i in range(slot_blocks):
            j = slot * slot_blocks + i
            for a in range(per_block):
                at = a * channels + group * GROUP_SIZE + above
                place = (j * per_block + a) * GROUP_SIZE + above
                code = results[group][place : place + 8, :]
                out_ref[j, at : at + 8, :] = code.astype(bf16)

    first_side([taps[pl.ds(g, SIDE, stride=groups), :] for g in range(groups)])
    turn(groups)
    spectra[...] = table_right(turned, second, groups).reshape(groups, SIDE, 2 * SIDE) * (
        1.0 / (SIDE * SIDE)
    )
    for n in range(LAGS - 1):
        step(n, n // slots, 0, tuple(n >= lag for lag in range(LAGS)))
        if n < slots:
            unpack(n, 1)

    def steady(n, carry):
        step(n, 1, 0)
        return carry

    lax.fori_loop(LAGS - 1, count, steady, 0)
    for n in range(count, count + LAGS - 1):
        step(n, 1, (n - 6) // slots, tuple(n - lag < count for lag in range(LAGS)))
        for slot in range(slots // 2):
            pack((n - count) % 2 * (slots // 2) + slot, (n - count) // 2)

    diagonal = lax.broadcasted_iota(jnp.int32, (channels, LANES), 1) == lax.broadcasted_iota(
        jnp.int32, (channels, LANES), 0
    )
    scale_row = jnp.sum(jnp.where(diagonal, units[...], 0.0), axis=0, keepdims=True)
    back_tails[pl.ds(0, blocks, stride=8), :] = jnp.broadcast_to(scale_row, (blocks, LANES))
    back_tails[pl.ds(7, blocks, stride=8), :] = jnp.zeros((blocks, LANES), f32)
    out_ref[:, data : data + 8, :] = back_tails[...].reshape(blocks, 8, LANES).astype(bf16)
    for slot in range(slots):
        pack(slot, 2 * groups - 1)
        out_copy(slot).start()
    for slot in range(slots):
        out_copy(slot).wait()


def local_kernel(q_ref, k_ref, v_ref, w_ref, skip_ref, q_out, s_out, ends_out, pads):
    rows, channels = q_ref.shape

    def column(block, carry):
        lanes = pl.ds(pl.multiple_of(block * LANES, LANES), LANES)
        for step in range(rows // SIDE):
            shorts = []
            for at, ref in enumerate((q_ref, k_ref, v_ref)):
                if step == 0:
                    before = jnp.zeros((8, LANES), f32)
                else:
                    before = ref[step * SIDE - 16 : step * SIDE, lanes].astype(f32)[8:]
                shorts.append(
                    short_conv(ref, step * SIDE, lanes, before, w_ref[at, :, lanes], pads.at[at])
                )
            if step == 0:
                ends_out[0:2, lanes] = shorts[1][0:2]
                ends_out[2:4, lanes] = shorts[2][0:2]
            span = slice(step * SIDE, (step + 1) * SIDE)
            q_out[span, lanes] = shorts[0]
            s_out[span, lanes] = skip_ref[:, lanes] * (shorts[1] * shorts[2])
        return carry

    ends_out[...] = jnp.zeros_like(ends_out)
    lax.fori_loop(0, channels // LANES, column, 0)


def join_kernel(
    in_ref, q_ref, s_ref, ends_ref, w_ref, skip_ref, out_hbm, out_buf, units, fixes, sems
):
    rows, channels = q_ref.shape
    blocks = channels // LANES
    sources = in_ref.shape[0] // blocks
    per = LANES // sources
    steps = rows // SIDE
    base = steps * per
    lane = lax.broadcasted_iota(jnp.int32, (8, LANES), 1)
    for block in range(blocks):
        lanes = slice(block * LANES, (block + 1) * LANES)
        tail = jnp.zeros((8, LANES), f32)
        for i in range(sources):
            part = in_ref[block * sources + i, base : base + 8, :].astype(f32)
            tail = jnp.where(lane // per == i, pltpu.roll(part, i * per, 1), tail)
        units[:, lanes] = tail[0:1] * (1.0 / CODE_TOP)
        adds = []
        for at in range(3):
            ago_2, ago_1 = tail[1 + 2 * at : 2 + 2 * at], tail[2 + 2 * at : 3 + 2 * at]
            weight_1, weight_2 = w_ref[at, 1:2, lanes], w_ref[at, 2:3, lanes]
            adds.append((weight_1 * ago_1 + weight_2 * ago_2, weight_2 * ago_1))
        for token in range(2):
            k_short = ends_ref[token : token + 1, lanes] + adds[1][token]
            v_short = ends_ref[2 + token : 3 + token, lanes] + adds[2][token]
            fixes[token : token + 1, lanes] = q_ref[token : token + 1, lanes] + adds[0][token]
            fixes[2 + token : 3 + token, lanes] = skip_ref[:, lanes] * (k_short * v_short)

    first_rows = lax.broadcasted_iota(jnp.int32, (8, LANES), 0) < 2
    copies = []
    for step in range(steps):
        span = slice(step * SIDE, (step + 1) * SIDE)

        for block in range(blocks):
            lanes = slice(block * LANES, (block + 1) * LANES)
            of_block = slice(block * sources, (block + 1) * sources)
            code = in_ref[of_block, step * per : (step + 1) * per, :]
            tile = code.astype(f32).reshape(LANES, SIDE).T
            long_conv = decode(tile, units[:, lanes])
            q_short, skipped = q_ref[span, lanes], s_ref[span, lanes]
            if step == 0:
                fix = fixes[:, lanes]
                q_start = jnp.where(first_rows, fix, q_short[:8])
                s_start = jnp.where(first_rows, pltpu.roll(fix, 6, 0), skipped[:8])
                q_short = jnp.concatenate([q_start, q_short[8:]], axis=0)
                skipped = jnp.concatenate([s_start, skipped[8:]], axis=0)
            out_buf[span, lanes] = (q_short * (long_conv + skipped)).astype(bf16)
        rows_at = pl.ds(step * SIDE, SIDE)
        copies.append(
            pltpu.make_async_copy(out_buf.at[rows_at], out_hbm.at[rows_at], sems.at[step])
        )
        copies[-1].start()
    for copy in copies:
        copy.wait()


def shards(query_in, key_in, value_in, short_weight, skip_bias, filter_taps):
    rows, channels = query_in.shape
    seq = lax.axis_size("seq")
    own = channels // seq
    blocks = channels // LANES
    groups = own // GROUP_SIZE
    sent = rows * own // LANES
    steps = rows // SIDE
    whole = pl.BlockSpec(memory_space=pltpu.VMEM)
    hbm = pl.BlockSpec(memory_space=pltpu.HBM)
    resident = pltpu.CompilerParams(vmem_limit_bytes=RESIDENT_LIMIT)
    streaming = pltpu.CompilerParams(vmem_limit_bytes=STREAMING_LIMIT)

    message = pl.pallas_call(
        gate_kernel,
        in_specs=[hbm] * 5,
        out_specs=hbm,
        out_shape=jax.ShapeDtypeStruct((seq, sent + 16, LANES), bf16),
        scratch_shapes=[
            pltpu.VMEM((rows, channels), bf16),
            pltpu.VMEM((rows, channels), bf16),
            pltpu.VMEM((16, channels), bf16),
            pltpu.VMEM(short_weight.shape, f32),
            pltpu.VMEM(filter_taps.shape, f32),
            pltpu.VMEM((seq, sent + 16, LANES), bf16),
            pltpu.VMEM((blocks, 2, 16 + SIDE, LANES), f32),
            pltpu.VMEM((8, channels), f32),
            pltpu.VMEM((blocks, 8, LANES), f32),
            pltpu.VMEM((blocks, 8, LANES), f32),
            pltpu.VMEM((blocks, 2 * steps * filter_taps.shape[0] // blocks, LANES), f32),
            pltpu.SemaphoreType.DMA((4, steps)),
            pltpu.SemaphoreType.DMA((blocks,)),
        ],
        compiler_params=streaming,
        name="gate",
    )(query_in, key_in, value_in, short_weight, filter_taps)
    message, query_in, key_in, value_in, short_weight, skip_bias, known = lax.optimization_barrier(
        (message, query_in, key_in, value_in, short_weight, skip_bias, table_blocks())
    )
    message = lax.all_to_all(message, "seq", 0, 0)

    q_short, skipped, ends = pl.pallas_call(
        local_kernel,
        in_specs=[whole] * 5,
        out_specs=[whole] * 3,
        out_shape=[
            jax.ShapeDtypeStruct((rows, channels), f32),
            jax.ShapeDtypeStruct((rows, channels), f32),
            jax.ShapeDtypeStruct((8, channels), f32),
        ],
        scratch_shapes=[pltpu.VMEM((3, 16 + SIDE, LANES), f32)],
        compiler_params=streaming,
        cost_estimate=pl.CostEstimate(
            flops=20 * rows * channels, bytes_accessed=14 * rows * channels, transcendentals=0
        ),
        name="local",
    )(query_in, key_in, value_in, short_weight, skip_bias[None])
    weights = lax.dynamic_slice_in_dim(short_weight, lax.axis_index("seq") * own, own, axis=2)
    weights = jnp.pad(weights, ((0, 0), (0, 0), (0, LANES - own)))
    message, q_short, skipped, ends, weights = lax.optimization_barrier(
        (message, q_short, skipped, ends, weights)
    )

    message = pl.pallas_call(
        mix_kernel,
        in_specs=[whole] * 3,
        out_specs=hbm,
        out_shape=jax.ShapeDtypeStruct((seq, sent + 8, LANES), bf16),
        scratch_shapes=[
            pltpu.VMEM((seq, sent + 8, LANES), bf16),
            *[pltpu.VMEM((seq * sent // groups, LANES), f32)] * (2 * groups),
            pltpu.VMEM((seq * 8, LANES), f32),
            pltpu.VMEM((groups, SIDE, 2 * SIDE), f32),
            pltpu.VMEM((own, LANES), f32),
            pltpu.VMEM((seq * 8, LANES), f32),
            pltpu.VMEM((seq * 8, LANES), f32),
            pltpu.VMEM((SIDE, LANES), f32),
            pltpu.VMEM((SIDE, LANES), f32),
            pltpu.VMEM((WIDE * SIDE, 4 * SIDE), bf16),
            pltpu.VMEM((WIDE * SIDE, 4 * SIDE), bf16),
            pltpu.VMEM((4 * SIDE, WIDE * SIDE), bf16),
            pltpu.VMEM((WIDE // 2, 2 * SIDE, 2 * SIDE), f32),
            pltpu.VMEM((WIDE * SIDE, 2 * SIDE), f32),
            pltpu.VMEM((WIDE // 2, SIDE, 2 * SIDE), f32),
            pltpu.VMEM((4 * SIDE, 2 * SIDE), bf16),
            pltpu.VMEM((6 * SIDE, 2 * SIDE), bf16),
            pltpu.VMEM((6 * SIDE, 2 * SIDE), bf16),
            pltpu.VMEM((2 * SIDE, 2 * SIDE), bf16),
            pltpu.VMEM((2, SIDE, LANES), f32),
            pltpu.SemaphoreType.DMA((own // WIDE // groups,)),
        ],
        compiler_params=pltpu.CompilerParams(vmem_limit_bytes=MIX_LIMIT),
        name="mix",
    )(message, weights, known)
    message = lax.all_to_all(message, "seq", 0, 0)

    return pl.pallas_call(
        join_kernel,
        in_specs=[whole] * 6,
        out_specs=hbm,
        out_shape=jax.ShapeDtypeStruct((rows, channels), bf16),
        scratch_shapes=[
            pltpu.VMEM((rows, channels), bf16),
            pltpu.VMEM((1, channels), f32),
            pltpu.VMEM((8, channels), f32),
            pltpu.SemaphoreType.DMA((steps,)),
        ],
        compiler_params=resident,
        name="join",
    )(message, q_short, skipped, ends, short_weight, skip_bias[None])


def solution(mesh):
    in_specs = (
        P("seq", "ch"),
        P("seq", "ch"),
        P("seq", "ch"),
        P(None, None, "ch"),
        P("ch"),
        P("ch", "seq"),
    )
    out_specs = P("seq", "ch")
    return jax.shard_map(shards, mesh=mesh, in_specs=in_specs, out_specs=out_specs, check_vma=False)
```

```python
import math

import jax
import jax.numpy as jnp
import numpy as np
from jax import lax
from jax.experimental import pallas as pl
from jax.experimental.pallas import tpu as pltpu
from jax.sharding import PartitionSpec as P

GROUP_SIZE = 16
SIDE = 128
LANES = 128
LAGS = 7
WIDE = 4
CODE_POWER = 17
CODE_TOP = 2.0 ** (120.0 / CODE_POWER)
CODE_LEAST = 2.0**-126
INV_LN2 = 1.0 / math.log(2.0)
RESIDENT_LIMIT = 12 * 1024 * 1024
MIX_LIMIT = 20 * 1024 * 1024
STREAMING_LIMIT = 60 * 1024 * 1024

f32, bf16 = jnp.float32, jnp.bfloat16


def encode(value, to_units):
    unit = value * to_units
    square = unit * unit
    fourth = square * square
    eighth = fourth * fourth
    return unit * (eighth * eighth)


def decode(code, from_units):
    size = jnp.maximum(jnp.abs(code), CODE_LEAST)
    root = jnp.exp2(jnp.log(size) * (INV_LN2 * (1.0 / CODE_POWER - 1.0)))
    return code * root * from_units


def code_scale(largest):
    return (jnp.maximum(largest, 1e-30) * 1.01).astype(bf16).astype(f32)


def table_blocks():
    side = np.arange(SIDE)
    inner = 2 * np.pi / SIDE * (side[:, None] * side[None, :] % SIDE)
    outer = 2 * np.pi / (4 * SIDE) * (side[None, :] * (4 * side[:, None] + 1) % (4 * SIDE))
    twist = 2 * np.pi / (4 * SIDE * SIDE) * (side[None, :] * (4 * side[:, None] + 1))
    blocks = []
    for angle in (inner, outer, outer.T, twist):
        for table in (np.cos(angle), np.sin(angle)):
            high = table.astype(jnp.bfloat16)
            blocks += [high, (table - high.astype(np.float64)).astype(jnp.bfloat16)]
    return np.concatenate(blocks, axis=0)


def dot(left, right):
    return jnp.dot(left, right, preferred_element_type=f32)


def halves(value):
    high = value.astype(bf16)
    return high, (value - high.astype(f32)).astype(bf16)


def short_conv(stream, at, lanes, before, weights, padded):
    now = stream[pl.ds(at, SIDE), lanes].astype(f32)
    padded[8:16, :] = before
    padded[16:, :] = now
    return (
        weights[0:1] * now
        + weights[1:2] * padded[15 : 15 + SIDE, :]
        + weights[2:3] * padded[14 : 14 + SIDE, :]
    )


def gate_kernel(
    q_hbm,
    k_hbm,
    v_hbm,
    w_hbm,
    taps_hbm,
    out_hbm,
    k_buf,
    v_buf,
    q_buf,
    w_buf,
    taps_buf,
    out_ref,
    pads,
    scales,
    ends,
    q_ends,
    taps_in,
    sems,
    last_sems,
):
    rows, channels = k_buf.shape
    steps = rows // SIDE
    blocks = channels // LANES
    dests = out_ref.shape[0] // blocks
    per = LANES // dests
    base = steps * per
    held = taps_buf.shape[0] // blocks
    groups = held // dests

    def stream_copy(at, step):
        source, target = ((k_hbm, k_buf), (v_hbm, v_buf))[at]
        span = pl.ds(step * SIDE, SIDE)
        return pltpu.make_async_copy(source.at[span], target.at[span], sems.at[at, step])

    def out_copy(step):
        span = pl.ds(step * per, per)
        return pltpu.make_async_copy(out_ref.at[:, span], out_hbm.at[:, span], sems.at[3, step])

    def last_copy(block):
        dest, span = pl.ds(block * dests, dests), pl.ds(base - per, per + 16)
        return pltpu.make_async_copy(
            out_ref.at[dest, span], out_hbm.at[dest, span], last_sems.at[block]
        )

    w_copy = pltpu.make_async_copy(w_hbm, w_buf, sems.at[2, 0])
    taps_copy = pltpu.make_async_copy(taps_hbm, taps_buf, sems.at[2, 1])
    q_copy = pltpu.make_async_copy(q_hbm.at[pl.ds(rows - 16, 16)], q_buf, sems.at[2, 2])
    for step in range(steps):
        for at in range(2):
            stream_copy(at, step).start()
        if step == 0:
            w_copy.start()
    taps_copy.start()
    q_copy.start()
    w_copy.wait()

    for step in range(steps):
        for at in range(2):
            stream_copy(at, step).wait()
        if step == steps - 1:
            taps_copy.wait()
            q_copy.wait()

        def tile(block, step=step):
            lanes = slice(block * LANES, (block + 1) * LANES)
            shorts = []
            for at, buf in enumerate((k_buf, v_buf)):
                if step == 0:
                    before = jnp.zeros((8, LANES), f32)
                else:
                    before = buf[step * SIDE - 16 : step * SIDE, lanes].astype(f32)[8:]
                shorts.append(
                    short_conv(
                        buf, step * SIDE, lanes, before, w_buf[1 + at, :, lanes], pads.at[block, at]
                    )
                )
            gated = shorts[0] * shorts[1]
            scale = code_scale(jnp.max(jnp.abs(gated), axis=0, keepdims=True))
            scales[step : step + 1, lanes] = scale
            code = encode(gated, CODE_TOP / scale).T.astype(bf16)
            span = slice(block * dests, (block + 1) * dests)
            out_ref[span, step * per : (step + 1) * per, :] = code.reshape(dests, per, LANES)

        if step < steps - 1:
            for block in range(blocks):
                tile(block)
            out_copy(step).start()

    def tail(block):
        slot = block
        lanes = slice(block * LANES, (block + 1) * LANES)
        for a in range(steps):
            taps_in[slot, a * held : (a + 1) * held, :] = taps_buf[
                block * held : (block + 1) * held, a * LANES : (a + 1) * LANES
            ]
        taps_at = steps * held
        for a in range(steps):
            for g in range(groups):
                piece = taps_in[slot, pl.ds(a * held + g, dests, stride=groups), :]
                taps_in[slot, pl.ds(taps_at + a * groups + g, dests, stride=8), :] = piece
        own_taps = taps_in[slot, taps_at:, :]
        taps_scale = code_scale(jnp.max(jnp.abs(own_taps), axis=1, keepdims=True))
        taps_code = encode(own_taps, CODE_TOP / taps_scale)
        taps_scale = jnp.broadcast_to(taps_scale, own_taps.shape)
        for at, buf in enumerate((k_buf, v_buf)):
            ends[slot, 4 * at : 4 * at + 2, :] = buf[rows - 16 :, lanes].astype(f32)[14:16]
            ends[slot, 4 * at + 2 : 4 * at + 4, :] = buf[0:16, lanes].astype(f32)[0:2]
        q_ends[slot, 0:2, :] = q_buf[:, lanes].astype(f32)[14:16]
        lane = lax.broadcasted_iota(jnp.int32, (8, LANES), 1)
        for d in range(dests):
            asked = pltpu.roll(q_ends[slot], (LANES + 3 * per - d * per) % LANES, 1)
            kept = pltpu.roll(ends[slot], (LANES - d * per) % LANES, 1)
            scaled = pltpu.roll(scales[:, lanes], (LANES + per - d * per) % LANES, 1)
            of_taps = taps_scale[8 * d : 8 * d + 8]
            last = jnp.where(lane < per, kept, jnp.where(lane < 2 * per, scaled, of_taps))
            last = jnp.where(lane < 3 * per, last, asked)
            both = jnp.concatenate([taps_code[8 * d : 8 * d + 8], last], axis=0).astype(bf16)
            out_ref[block * dests + d, base : base + 16, :] = both

    scales[steps:, :] = jnp.zeros((8 - steps, channels), f32)
    q_ends[...] = jnp.zeros_like(q_ends)
    for block in range(blocks):
        tile(block)
        tail(block)
        if block % 2 == 1:
            last_copy(block - 1).start()
            last_copy(block).start()
    for step in range(steps - 1):
        out_copy(step).wait()
    for block in range(blocks):
        last_copy(block).wait()


def mix_kernel(
    in_ref,
    w_ref,
    table_ref,
    out_hbm,
    out_ref,
    signal_0,
    signal_1,
    result_0,
    result_1,
    taps,
    spectra,
    units,
    tails,
    back_tails,
    levels,
    starts,
    turned,
    filtered,
    unturned,
    first_raw,
    third_raw,
    fourth_raw,
    first,
    second,
    third,
    fourth,
    twist,
    out_sems,
):
    signals, results = (signal_0, signal_1), (result_0, result_1)
    groups = len(signals)
    blocks = in_ref.shape[0]
    per_block = SIDE // blocks
    channels = groups * GROUP_SIZE
    data = per_block * channels
    count = channels // WIDE
    slots = count // groups
    slot_blocks = blocks // slots

    def out_copy(slot):
        span = pl.ds(slot * slot_blocks, slot_blocks)
        return pltpu.make_async_copy(out_ref.at[span], out_hbm.at[span], out_sems.at[slot])

    def unpack(slot, group):
        for i in range(slot_blocks):
            j = slot * slot_blocks + i
            for a in range(per_block):
                at = a * channels + group * GROUP_SIZE
                place = (j * per_block + a) * GROUP_SIZE
                code = in_ref[j, at : at + GROUP_SIZE, :].astype(f32)
                signals[group][place : place + GROUP_SIZE, :] = code

    for slot in range(slots):
        unpack(slot, 0)

    def block(at):
        return table_ref[at * SIDE : (at + 1) * SIDE, :]

    for part in range(2):
        inner_cos, inner_sin = block(part), block(2 + part)
        for at in ((0, 2 * SIDE), (4 * SIDE,))[part]:
            second[at : at + SIDE, :SIDE] = inner_cos
            second[at : at + SIDE, SIDE:] = -inner_sin
            second[at + SIDE : at + 2 * SIDE, :SIDE] = inner_sin
            second[at + SIDE : at + 2 * SIDE, SIDE:] = inner_cos
            third[at : at + SIDE, :SIDE] = inner_cos
            third[at : at + SIDE, SIDE:] = inner_sin
            third[at + SIDE : at + 2 * SIDE, :SIDE] = -inner_sin
            third[at + SIDE : at + 2 * SIDE, SIDE:] = inner_cos
        at = 2 * part * SIDE
        for span in (slice(0, SIDE), slice(SIDE, 2 * SIDE)):
            first[at : at + SIDE, span] = block(4 + part)
            first[at + SIDE : at + 2 * SIDE, span] = -block(6 + part)
        fourth[part * SIDE : (part + 1) * SIDE, :SIDE] = block(8 + part)
        fourth[part * SIDE : (part + 1) * SIDE, SIDE:] = -block(10 + part)
        twist[part] = block(12 + 2 * part).astype(f32) + block(13 + 2 * part).astype(f32)

    of_message = in_ref[:, data : data + 16, :].astype(f32)
    tails[...] = of_message[:, 8:].reshape(blocks * 8, LANES)
    taps_code = of_message[:, :8].reshape(blocks * 8, LANES)
    taps[...] = decode(taps_code, 1.0 / CODE_TOP) * tails[:, 2 * channels : 2 * channels + 1]
    for a in range(per_block):
        levels[pl.ds(a, blocks, stride=per_block), :] = tails[pl.ds(a, blocks, stride=8), :]

    def gated_starts():
        block = lax.broadcasted_iota(jnp.int32, (blocks, LANES), 0)
        shorts = []
        for at in range(2):
            ago_2, ago_1, now, later = [
                tails[pl.ds(4 * at + i, blocks, stride=8), :] for i in range(4)
            ]
            ago_2 = jnp.where(block == 0, 0.0, pltpu.roll(ago_2, 1, 0))
            ago_1 = jnp.where(block == 0, 0.0, pltpu.roll(ago_1, 1, 0))
            back_tails[pl.ds(3 + 2 * at, blocks, stride=8), :] = ago_2
            back_tails[pl.ds(4 + 2 * at, blocks, stride=8), :] = ago_1
            taps_0, taps_1, taps_2 = [w_ref[1 + at, i : i + 1, :] for i in range(3)]
            shorts.append(
                (
                    taps_0 * now + taps_1 * ago_1 + taps_2 * ago_2,
                    taps_0 * later + taps_1 * now + taps_2 * ago_1,
                )
            )
        for at in range(2):
            asked = pltpu.roll(tails[pl.ds(at, blocks, stride=8), :], LANES - 3 * channels, 1)
            asked = jnp.where(block == 0, 0.0, pltpu.roll(asked, 1, 0))
            back_tails[pl.ds(1 + at, blocks, stride=8), :] = asked
        from_lane = lax.broadcasted_iota(jnp.int32, (LANES, LANES), 0)
        to_lane = lax.broadcasted_iota(jnp.int32, (LANES, LANES), 1)
        known = lax.broadcasted_iota(jnp.int32, (blocks, LANES), 1) < channels
        spread = jnp.zeros((blocks, LANES), f32)
        for token in range(2):
            gated = jnp.where(known, shorts[0][token] * shorts[1][token], 0.0)
            place = jnp.where(to_lane == 2 * from_lane + token, 1.0, 0.0).astype(bf16)
            for part in halves(gated):
                spread = spread + dot(part, place)
        starts[...] = jnp.zeros((SIDE, LANES), f32)
        starts[pl.ds(0, blocks, stride=per_block), :] = spread

    gated_starts()

    cos, sin = twist[0], twist[1]

    def store_halves(ref, at, value):
        high, low = halves(value)
        ref[at * SIDE : (at + 1) * SIDE, : 2 * SIDE] = high
        ref[at * SIDE : (at + 1) * SIDE, 2 * SIDE :] = low

    def table_right(ref, table, used=WIDE):
        rows = used * SIDE
        return dot(ref[:rows], table[: 4 * SIDE]) + dot(ref[:rows, : 2 * SIDE], table[4 * SIDE :])

    lane = lax.broadcasted_iota(jnp.int32, (SIDE, LANES), 1)
    is_start = (lax.broadcasted_iota(jnp.int32, (SIDE, LANES), 0) % per_block == 0) & (lane < 2)

    def load(n, group):
        level = pltpu.roll(levels[...], LANES - channels - WIDE * n, 1) * (1.0 / CODE_TOP)
        at = WIDE * (n - group * slots)
        values = []
        for i in range(WIDE):
            code = signals[group][pl.ds(at + i, SIDE, stride=GROUP_SIZE), :]
            value = decode(code, level[:, i : i + 1])
            start = pltpu.roll(starts[...], (LANES - 2 * (WIDE * n + i)) % LANES, 1)
            values.append(jnp.where(is_start, start, value))
        return values

    def first_side(values):
        for pair in range(len(values) // 2):
            high, low = halves(jnp.concatenate(values[2 * pair : 2 * pair + 2], axis=1))
            both = jnp.concatenate([high, low], axis=0)
            first_raw[pair] = dot(first[: 2 * SIDE], both) + dot(first[2 * SIDE :, :SIDE], high)

    def turn(used=WIDE):
        for at in range(used):
            span = slice(at % 2 * SIDE, (at % 2 + 1) * SIDE)
            re, im = first_raw[at // 2, :SIDE, span], first_raw[at // 2, SIDE:, span]
            store_halves(
                turned, at, jnp.concatenate([re * cos + im * sin, im * cos - re * sin], axis=1)
            )

    def filter_spectrum(n, spectrum):
        of_taps = spectra[WIDE * n // GROUP_SIZE]
        f_re, f_im = of_taps[:, :SIDE], of_taps[:, SIDE:]
        for at in range(WIDE):
            s_re = spectrum[at * SIDE : (at + 1) * SIDE, :SIDE]
            s_im = spectrum[at * SIDE : (at + 1) * SIDE, SIDE:]
            store_halves(
                filtered,
                at,
                jnp.concatenate([s_re * f_re - s_im * f_im, s_re * f_im + s_im * f_re], axis=1),
            )

    def turn_back():
        for at in range(WIDE):
            re = third_raw[at * SIDE : (at + 1) * SIDE, :SIDE]
            im = third_raw[at * SIDE : (at + 1) * SIDE, SIDE:]
            high, low = halves(jnp.concatenate([re * cos - im * sin, im * cos + re * sin], axis=0))
            unturned[: 2 * SIDE, at * SIDE : (at + 1) * SIDE] = high
            unturned[2 * SIDE :, at * SIDE : (at + 1) * SIDE] = low

    def first_side_back():
        for pair in range(WIDE // 2):
            span = slice(2 * pair * SIDE, (2 * pair + 2) * SIDE)
            done = dot(fourth[...], unturned[: 2 * SIDE, span])
            fourth_raw[pair] = (
                done[:SIDE] + done[SIDE:] + dot(fourth[:SIDE], unturned[2 * SIDE :, span])
            )

    def finish(n, group):
        for i in range(WIDE):
            value = fourth_raw[i // 2, :, i % 2 * SIDE : (i % 2 + 1) * SIDE]
            top = jnp.max(jnp.max(jnp.abs(value), axis=0, keepdims=True), axis=1, keepdims=True)
            scale = code_scale(top)
            channel = WIDE * n + i
            units[pl.ds(channel, 1), :] = jnp.broadcast_to(scale, (1, LANES))
            place = pl.ds(channel - group * GROUP_SIZE, SIDE, stride=GROUP_SIZE)
            results[group][place, :] = encode(value, CODE_TOP / scale)

    def step(n, load_group, finish_group, active=(True,) * LAGS):
        loads, turns, filters, filtered_back, turns_back, sides_back, finishes = active
        if finishes:
            finish(n - 6, finish_group)
        if sides_back:
            first_side_back()
        if turns_back:
            turn_back()
        if filters:
            spectrum = table_right(turned, second)
        if turns:
            turn()
        if filtered_back:
            third_raw[...] = table_right(filtered, third)
        if filters:
            filter_spectrum(n - 2, spectrum)
        if loads:
            first_side(load(n, load_group))

    def pack(slot, half):
        group, above = half // 2, half % 2 * 8
        for i in range(slot_blocks):
            j = slot * slot_blocks + i
            for a in range(per_block):
                at = a * channels + group * GROUP_SIZE + above
                place = (j * per_block + a) * GROUP_SIZE + above
                code = results[group][place : place + 8, :]
                out_ref[j, at : at + 8, :] = code.astype(bf16)

    first_side([taps[pl.ds(g, SIDE, stride=groups), :] for g in range(groups)])
    turn(groups)
    spectra[...] = table_right(turned, second, groups).reshape(groups, SIDE, 2 * SIDE) * (
        1.0 / (SIDE * SIDE)
    )
    for n in range(LAGS - 1):
        step(n, n // slots, 0, tuple(n >= lag for lag in range(LAGS)))
        if n < slots:
            unpack(n, 1)

    for n in range(LAGS - 1, count):
        step(n, 1, 0)
    for n in range(count, count + LAGS - 1):
        step(n, 1, (n - 6) // slots, tuple(n - lag < count for lag in range(LAGS)))
        for slot in range(slots // 2):
            pack((n - count) % 2 * (slots // 2) + slot, (n - count) // 2)

    diagonal = lax.broadcasted_iota(jnp.int32, (channels, LANES), 1) == lax.broadcasted_iota(
        jnp.int32, (channels, LANES), 0
    )
    scale_row = jnp.sum(jnp.where(diagonal, units[...], 0.0), axis=0, keepdims=True)
    back_tails[pl.ds(0, blocks, stride=8), :] = jnp.broadcast_to(scale_row, (blocks, LANES))
    back_tails[pl.ds(7, blocks, stride=8), :] = jnp.zeros((blocks, LANES), f32)
    out_ref[:, data : data + 8, :] = back_tails[...].reshape(blocks, 8, LANES).astype(bf16)
    for slot in range(slots):
        pack(slot, 2 * groups - 1)
        out_copy(slot).start()
    for slot in range(slots):
        out_copy(slot).wait()


def local_kernel(q_ref, k_ref, v_ref, w_ref, skip_ref, q_out, s_out, ends_out, pads):
    rows, channels = q_ref.shape

    def column(block, carry):
        lanes = pl.ds(pl.multiple_of(block * LANES, LANES), LANES)
        for step in range(rows // SIDE):
            shorts = []
            for at, ref in enumerate((q_ref, k_ref, v_ref)):
                if step == 0:
                    before = jnp.zeros((8, LANES), f32)
                else:
                    before = ref[step * SIDE - 16 : step * SIDE, lanes].astype(f32)[8:]
                shorts.append(
                    short_conv(ref, step * SIDE, lanes, before, w_ref[at, :, lanes], pads.at[at])
                )
            if step == 0:
                ends_out[0:2, lanes] = shorts[1][0:2]
                ends_out[2:4, lanes] = shorts[2][0:2]
            span = slice(step * SIDE, (step + 1) * SIDE)
            q_out[span, lanes] = shorts[0]
            s_out[span, lanes] = skip_ref[:, lanes] * (shorts[1] * shorts[2])
        return carry

    ends_out[...] = jnp.zeros_like(ends_out)
    lax.fori_loop(0, channels // LANES, column, 0)


def join_kernel(
    in_ref, q_ref, s_ref, ends_ref, w_ref, skip_ref, out_hbm, out_buf, units, fixes, sems
):
    rows, channels = q_ref.shape
    blocks = channels // LANES
    sources = in_ref.shape[0] // blocks
    per = LANES // sources
    steps = rows // SIDE
    base = steps * per
    lane = lax.broadcasted_iota(jnp.int32, (8, LANES), 1)
    for block in range(blocks):
        lanes = slice(block * LANES, (block + 1) * LANES)
        tail = jnp.zeros((8, LANES), f32)
        for i in range(sources):
            part = in_ref[block * sources + i, base : base + 8, :].astype(f32)
            tail = jnp.where(lane // per == i, pltpu.roll(part, i * per, 1), tail)
        units[:, lanes] = tail[0:1] * (1.0 / CODE_TOP)
        adds = []
        for at in range(3):
            ago_2, ago_1 = tail[1 + 2 * at : 2 + 2 * at], tail[2 + 2 * at : 3 + 2 * at]
            weight_1, weight_2 = w_ref[at, 1:2, lanes], w_ref[at, 2:3, lanes]
            adds.append((weight_1 * ago_1 + weight_2 * ago_2, weight_2 * ago_1))
        for token in range(2):
            k_short = ends_ref[token : token + 1, lanes] + adds[1][token]
            v_short = ends_ref[2 + token : 3 + token, lanes] + adds[2][token]
            fixes[token : token + 1, lanes] = q_ref[token : token + 1, lanes] + adds[0][token]
            fixes[2 + token : 3 + token, lanes] = skip_ref[:, lanes] * (k_short * v_short)

    first_rows = lax.broadcasted_iota(jnp.int32, (8, LANES), 0) < 2
    copies = []
    for step in range(steps):
        span = slice(step * SIDE, (step + 1) * SIDE)

        for block in range(blocks):
            lanes = slice(block * LANES, (block + 1) * LANES)
            of_block = slice(block * sources, (block + 1) * sources)
            code = in_ref[of_block, step * per : (step + 1) * per, :]
            tile = code.astype(f32).reshape(LANES, SIDE).T
            long_conv = decode(tile, units[:, lanes])
            q_short, skipped = q_ref[span, lanes], s_ref[span, lanes]
            if step == 0:
                fix = fixes[:, lanes]
                q_start = jnp.where(first_rows, fix, q_short[:8])
                s_start = jnp.where(first_rows, pltpu.roll(fix, 6, 0), skipped[:8])
                q_short = jnp.concatenate([q_start, q_short[8:]], axis=0)
                skipped = jnp.concatenate([s_start, skipped[8:]], axis=0)
            out_buf[span, lanes] = (q_short * (long_conv + skipped)).astype(bf16)
        rows_at = pl.ds(step * SIDE, SIDE)
        copies.append(
            pltpu.make_async_copy(out_buf.at[rows_at], out_hbm.at[rows_at], sems.at[step])
        )
        copies[-1].start()
    for copy in copies:
        copy.wait()


def shards(query_in, key_in, value_in, short_weight, skip_bias, filter_taps):
    rows, channels = query_in.shape
    seq = lax.axis_size("seq")
    own = channels // seq
    blocks = channels // LANES
    groups = own // GROUP_SIZE
    sent = rows * own // LANES
    steps = rows // SIDE
    whole = pl.BlockSpec(memory_space=pltpu.VMEM)
    hbm = pl.BlockSpec(memory_space=pltpu.HBM)
    resident = pltpu.CompilerParams(vmem_limit_bytes=RESIDENT_LIMIT)
    streaming = pltpu.CompilerParams(vmem_limit_bytes=STREAMING_LIMIT)

    message = pl.pallas_call(
        gate_kernel,
        in_specs=[hbm] * 5,
        out_specs=hbm,
        out_shape=jax.ShapeDtypeStruct((seq, sent + 16, LANES), bf16),
        scratch_shapes=[
            pltpu.VMEM((rows, channels), bf16),
            pltpu.VMEM((rows, channels), bf16),
            pltpu.VMEM((16, channels), bf16),
            pltpu.VMEM(short_weight.shape, f32),
            pltpu.VMEM(filter_taps.shape, f32),
            pltpu.VMEM((seq, sent + 16, LANES), bf16),
            pltpu.VMEM((blocks, 2, 16 + SIDE, LANES), f32),
            pltpu.VMEM((8, channels), f32),
            pltpu.VMEM((blocks, 8, LANES), f32),
            pltpu.VMEM((blocks, 8, LANES), f32),
            pltpu.VMEM((blocks + 1, 2 * steps * filter_taps.shape[0] // blocks, LANES), f32),
            pltpu.SemaphoreType.DMA((4, steps)),
            pltpu.SemaphoreType.DMA((blocks,)),
        ],
        compiler_params=streaming,
        name="gate",
    )(query_in, key_in, value_in, short_weight, filter_taps)
    message, query_in, key_in, value_in, short_weight, skip_bias, known = lax.optimization_barrier(
        (message, query_in, key_in, value_in, short_weight, skip_bias, table_blocks())
    )
    message = lax.all_to_all(message, "seq", 0, 0)

    q_short, skipped, ends = pl.pallas_call(
        local_kernel,
        in_specs=[whole] * 5,
        out_specs=[whole] * 3,
        out_shape=[
            jax.ShapeDtypeStruct((rows, channels), f32),
            jax.ShapeDtypeStruct((rows, channels), f32),
            jax.ShapeDtypeStruct((8, channels), f32),
        ],
        scratch_shapes=[pltpu.VMEM((3, 16 + SIDE, LANES), f32)],
        compiler_params=streaming,
        cost_estimate=pl.CostEstimate(
            flops=20 * rows * channels, bytes_accessed=14 * rows * channels, transcendentals=0
        ),
        name="local",
    )(query_in, key_in, value_in, short_weight, skip_bias[None])
    weights = lax.dynamic_slice_in_dim(short_weight, lax.axis_index("seq") * own, own, axis=2)
    weights = jnp.pad(weights, ((0, 0), (0, 0), (0, LANES - own)))
    message, q_short, skipped, ends, weights = lax.optimization_barrier(
        (message, q_short, skipped, ends, weights)
    )

    message = pl.pallas_call(
        mix_kernel,
        in_specs=[whole] * 3,
        out_specs=hbm,
        out_shape=jax.ShapeDtypeStruct((seq, sent + 8, LANES), bf16),
        scratch_shapes=[
            pltpu.VMEM((seq, sent + 8, LANES), bf16),
            *[pltpu.VMEM((seq * sent // groups, LANES), f32)] * (2 * groups),
            pltpu.VMEM((seq * 8, LANES), f32),
            pltpu.VMEM((groups, SIDE, 2 * SIDE), f32),
            pltpu.VMEM((own, LANES), f32),
            pltpu.VMEM((seq * 8, LANES), f32),
            pltpu.VMEM((seq * 8, LANES), f32),
            pltpu.VMEM((SIDE, LANES), f32),
            pltpu.VMEM((SIDE, LANES), f32),
            pltpu.VMEM((WIDE * SIDE, 4 * SIDE), bf16),
            pltpu.VMEM((WIDE * SIDE, 4 * SIDE), bf16),
            pltpu.VMEM((4 * SIDE, WIDE * SIDE), bf16),
            pltpu.VMEM((WIDE // 2, 2 * SIDE, 2 * SIDE), f32),
            pltpu.VMEM((WIDE * SIDE, 2 * SIDE), f32),
            pltpu.VMEM((WIDE // 2, SIDE, 2 * SIDE), f32),
            pltpu.VMEM((4 * SIDE, 2 * SIDE), bf16),
            pltpu.VMEM((6 * SIDE, 2 * SIDE), bf16),
            pltpu.VMEM((6 * SIDE, 2 * SIDE), bf16),
            pltpu.VMEM((2 * SIDE, 2 * SIDE), bf16),
            pltpu.VMEM((2, SIDE, LANES), f32),
            pltpu.SemaphoreType.DMA((own // WIDE // groups,)),
        ],
        compiler_params=pltpu.CompilerParams(vmem_limit_bytes=MIX_LIMIT),
        name="mix",
    )(message, weights, known)
    message = lax.all_to_all(message, "seq", 0, 0)

    return pl.pallas_call(
        join_kernel,
        in_specs=[whole] * 6,
        out_specs=hbm,
        out_shape=jax.ShapeDtypeStruct((rows, channels), bf16),
        scratch_shapes=[
            pltpu.VMEM((rows, channels), bf16),
            pltpu.VMEM((1, channels), f32),
            pltpu.VMEM((8, channels), f32),
            pltpu.SemaphoreType.DMA((steps,)),
        ],
        compiler_params=resident,
        name="join",
    )(message, q_short, skipped, ends, short_weight, skip_bias[None])


def solution(mesh):
    in_specs = (
        P("seq", "ch"),
        P("seq", "ch"),
        P("seq", "ch"),
        P(None, None, "ch"),
        P("ch"),
        P("ch", "seq"),
    )
    out_specs = P("seq", "ch")
    return jax.shard_map(shards, mesh=mesh, in_specs=in_specs, out_specs=out_specs, check_vma=False)
```

```python
import math

import jax
import jax.numpy as jnp
import numpy as np
from jax import lax
from jax.experimental import pallas as pl
from jax.experimental.pallas import tpu as pltpu
from jax.sharding import PartitionSpec as P

GROUP_SIZE = 16
SIDE = 128
LANES = 128
LAGS = 7
WIDE = 4
CODE_POWER = 17
CODE_TOP = 2.0 ** (120.0 / CODE_POWER)
CODE_LEAST = 2.0**-126
INV_LN2 = 1.0 / math.log(2.0)
RESIDENT_LIMIT = 12 * 1024 * 1024
MIX_LIMIT = 20 * 1024 * 1024
STREAMING_LIMIT = 60 * 1024 * 1024

f32, bf16 = jnp.float32, jnp.bfloat16


def encode(value, to_units):
    unit = value * to_units
    square = unit * unit
    fourth = square * square
    eighth = fourth * fourth
    return unit * (eighth * eighth)


def decode(code, from_units):
    size = jnp.maximum(jnp.abs(code), CODE_LEAST)
    root = jnp.exp2(jnp.log(size) * (INV_LN2 * (1.0 / CODE_POWER - 1.0)))
    return code * root * from_units


def code_scale(largest):
    return (jnp.maximum(largest, 1e-30) * 1.01).astype(bf16).astype(f32)


def table_blocks():
    side = np.arange(SIDE)
    inner = 2 * np.pi / SIDE * (side[:, None] * side[None, :] % SIDE)
    outer = 2 * np.pi / (4 * SIDE) * (side[None, :] * (4 * side[:, None] + 1) % (4 * SIDE))
    twist = 2 * np.pi / (4 * SIDE * SIDE) * (side[None, :] * (4 * side[:, None] + 1))
    blocks = []
    for angle in (inner, outer, outer.T, twist):
        for table in (np.cos(angle), np.sin(angle)):
            high = table.astype(jnp.bfloat16)
            blocks += [high, (table - high.astype(np.float64)).astype(jnp.bfloat16)]
    return np.concatenate(blocks, axis=0)


def dot(left, right):
    return jnp.dot(left, right, preferred_element_type=f32)


def halves(value):
    high = value.astype(bf16)
    return high, (value - high.astype(f32)).astype(bf16)


def short_conv(stream, at, lanes, before, weights, padded):
    now = stream[pl.ds(at, SIDE), lanes].astype(f32)
    padded[8:16, :] = before
    padded[16:, :] = now
    return (
        weights[0:1] * now
        + weights[1:2] * padded[15 : 15 + SIDE, :]
        + weights[2:3] * padded[14 : 14 + SIDE, :]
    )


def gate_kernel(
    q_hbm,
    k_hbm,
    v_hbm,
    w_hbm,
    taps_hbm,
    out_hbm,
    k_buf,
    v_buf,
    q_buf,
    w_buf,
    taps_buf,
    out_ref,
    pads,
    scales,
    ends,
    q_ends,
    taps_in,
    sems,
    last_sems,
):
    rows, channels = k_buf.shape
    steps = rows // SIDE
    blocks = channels // LANES
    dests = out_ref.shape[0] // blocks
    per = LANES // dests
    base = steps * per
    held = taps_buf.shape[0] // blocks
    groups = held // dests

    def stream_copy(at, step):
        source, target = ((k_hbm, k_buf), (v_hbm, v_buf))[at]
        span = pl.ds(step * SIDE, SIDE)
        return pltpu.make_async_copy(source.at[span], target.at[span], sems.at[at, step])

    def out_copy(step):
        span = pl.ds(step * per, per)
        return pltpu.make_async_copy(out_ref.at[:, span], out_hbm.at[:, span], sems.at[3, step])

    def last_copy(block):
        dest, span = pl.ds(block * dests, dests), pl.ds(base - per, per + 16)
        return pltpu.make_async_copy(
            out_ref.at[dest, span], out_hbm.at[dest, span], last_sems.at[block]
        )

    w_copy = pltpu.make_async_copy(w_hbm, w_buf, sems.at[2, 0])
    taps_copy = pltpu.make_async_copy(taps_hbm, taps_buf, sems.at[2, 1])
    q_copy = pltpu.make_async_copy(q_hbm.at[pl.ds(rows - 16, 16)], q_buf, sems.at[2, 2])
    for step in range(steps):
        for at in range(2):
            stream_copy(at, step).start()
        if step == 0:
            w_copy.start()
    taps_copy.start()
    q_copy.start()
    w_copy.wait()

    for step in range(steps):
        for at in range(2):
            stream_copy(at, step).wait()
        if step == steps - 1:
            taps_copy.wait()
            q_copy.wait()

        def tile(block, step=step):
            lanes = slice(block * LANES, (block + 1) * LANES)
            shorts = []
            for at, buf in enumerate((k_buf, v_buf)):
                if step == 0:
                    before = jnp.zeros((8, LANES), f32)
                else:
                    before = buf[step * SIDE - 16 : step * SIDE, lanes].astype(f32)[8:]
                shorts.append(
                    short_conv(
                        buf, step * SIDE, lanes, before, w_buf[1 + at, :, lanes], pads.at[block, at]
                    )
                )
            gated = shorts[0] * shorts[1]
            scale = code_scale(jnp.max(jnp.abs(gated), axis=0, keepdims=True))
            scales[step : step + 1, lanes] = scale
            code = encode(gated, CODE_TOP / scale).T.astype(bf16)
            span = slice(block * dests, (block + 1) * dests)
            out_ref[span, step * per : (step + 1) * per, :] = code.reshape(dests, per, LANES)

        if step < steps - 1:
            for block in range(blocks):
                tile(block)
            out_copy(step).start()

    def tail(block):
        slot = block
        lanes = slice(block * LANES, (block + 1) * LANES)
        for a in range(steps):
            taps_in[slot, a * held : (a + 1) * held, :] = taps_buf[
                block * held : (block + 1) * held, a * LANES : (a + 1) * LANES
            ]
        taps_at = steps * held
        for a in range(steps):
            for g in range(groups):
                piece = taps_in[slot, pl.ds(a * held + g, dests, stride=groups), :]
                taps_in[slot, pl.ds(taps_at + a * groups + g, dests, stride=8), :] = piece
        own_taps = taps_in[slot, taps_at:, :]
        taps_scale = code_scale(jnp.max(jnp.abs(own_taps), axis=1, keepdims=True))
        taps_code = encode(own_taps, CODE_TOP / taps_scale)
        taps_scale = jnp.broadcast_to(taps_scale, own_taps.shape)
        for at, buf in enumerate((k_buf, v_buf)):
            ends[slot, 4 * at : 4 * at + 2, :] = buf[rows - 16 :, lanes].astype(f32)[14:16]
            ends[slot, 4 * at + 2 : 4 * at + 4, :] = buf[0:16, lanes].astype(f32)[0:2]
        q_ends[slot, 0:2, :] = q_buf[:, lanes].astype(f32)[14:16]
        lane = lax.broadcasted_iota(jnp.int32, (8, LANES), 1)
        for d in range(dests):
            asked = pltpu.roll(q_ends[slot], (LANES + 3 * per - d * per) % LANES, 1)
            kept = pltpu.roll(ends[slot], (LANES - d * per) % LANES, 1)
            scaled = pltpu.roll(scales[:, lanes], (LANES + per - d * per) % LANES, 1)
            of_taps = taps_scale[8 * d : 8 * d + 8]
            last = jnp.where(lane < per, kept, jnp.where(lane < 2 * per, scaled, of_taps))
            last = jnp.where(lane < 3 * per, last, asked)
            both = jnp.concatenate([taps_code[8 * d : 8 * d + 8], last], axis=0).astype(bf16)
            out_ref[block * dests + d, base : base + 16, :] = both

    scales[steps:, :] = jnp.zeros((8 - steps, channels), f32)
    q_ends[...] = jnp.zeros_like(q_ends)
    for block in range(blocks):
        tile(block)
        tail(block)
        if block % 4 == 3:
            for at in range(block - 3, block + 1):
                last_copy(at).start()
    for step in range(steps - 1):
        out_copy(step).wait()
    for block in range(blocks):
        last_copy(block).wait()


def mix_kernel(
    in_ref,
    w_ref,
    table_ref,
    out_hbm,
    out_ref,
    signal_0,
    signal_1,
    result_0,
    result_1,
    taps,
    spectra,
    units,
    tails,
    back_tails,
    levels,
    starts,
    turned,
    filtered,
    unturned,
    first_raw,
    third_raw,
    fourth_raw,
    first,
    second,
    third,
    fourth,
    twist,
    out_sems,
):
    signals, results = (signal_0, signal_1), (result_0, result_1)
    groups = len(signals)
    blocks = in_ref.shape[0]
    per_block = SIDE // blocks
    channels = groups * GROUP_SIZE
    data = per_block * channels
    count = channels // WIDE
    slots = count // groups
    slot_blocks = blocks // slots

    def out_copy(slot):
        span = pl.ds(slot * slot_blocks, slot_blocks)
        return pltpu.make_async_copy(out_ref.at[span], out_hbm.at[span], out_sems.at[slot])

    def unpack(slot, group):
        for i in range(slot_blocks):
            j = slot * slot_blocks + i
            for a in range(per_block):
                at = a * channels + group * GROUP_SIZE
                place = (j * per_block + a) * GROUP_SIZE
                code = in_ref[j, at : at + GROUP_SIZE, :].astype(f32)
                signals[group][place : place + GROUP_SIZE, :] = code

    for slot in range(slots):
        unpack(slot, 0)

    def block(at):
        return table_ref[at * SIDE : (at + 1) * SIDE, :]

    for part in range(2):
        inner_cos, inner_sin = block(part), block(2 + part)
        for at in ((0, 2 * SIDE), (4 * SIDE,))[part]:
            second[at : at + SIDE, :SIDE] = inner_cos
            second[at : at + SIDE, SIDE:] = -inner_sin
            second[at + SIDE : at + 2 * SIDE, :SIDE] = inner_sin
            second[at + SIDE : at + 2 * SIDE, SIDE:] = inner_cos
            third[at : at + SIDE, :SIDE] = inner_cos
            third[at : at + SIDE, SIDE:] = inner_sin
            third[at + SIDE : at + 2 * SIDE, :SIDE] = -inner_sin
            third[at + SIDE : at + 2 * SIDE, SIDE:] = inner_cos
        at = 2 * part * SIDE
        for span in (slice(0, SIDE), slice(SIDE, 2 * SIDE)):
            first[at : at + SIDE, span] = block(4 + part)
            first[at + SIDE : at + 2 * SIDE, span] = -block(6 + part)
        fourth[part * SIDE : (part + 1) * SIDE, :SIDE] = block(8 + part)
        fourth[part * SIDE : (part + 1) * SIDE, SIDE:] = -block(10 + part)
        twist[part] = block(12 + 2 * part).astype(f32) + block(13 + 2 * part).astype(f32)

    of_message = in_ref[:, data : data + 16, :].astype(f32)
    tails[...] = of_message[:, 8:].reshape(blocks * 8, LANES)
    taps_code = of_message[:, :8].reshape(blocks * 8, LANES)
    taps[...] = decode(taps_code, 1.0 / CODE_TOP) * tails[:, 2 * channels : 2 * channels + 1]
    for a in range(per_block):
        levels[pl.ds(a, blocks, stride=per_block), :] = tails[pl.ds(a, blocks, stride=8), :]

    def gated_starts():
        block = lax.broadcasted_iota(jnp.int32, (blocks, LANES), 0)
        shorts = []
        for at in range(2):
            ago_2, ago_1, now, later = [
                tails[pl.ds(4 * at + i, blocks, stride=8), :] for i in range(4)
            ]
            ago_2 = jnp.where(block == 0, 0.0, pltpu.roll(ago_2, 1, 0))
            ago_1 = jnp.where(block == 0, 0.0, pltpu.roll(ago_1, 1, 0))
            back_tails[pl.ds(3 + 2 * at, blocks, stride=8), :] = ago_2
            back_tails[pl.ds(4 + 2 * at, blocks, stride=8), :] = ago_1
            taps_0, taps_1, taps_2 = [w_ref[1 + at, i : i + 1, :] for i in range(3)]
            shorts.append(
                (
                    taps_0 * now + taps_1 * ago_1 + taps_2 * ago_2,
                    taps_0 * later + taps_1 * now + taps_2 * ago_1,
                )
            )
        for at in range(2):
            asked = pltpu.roll(tails[pl.ds(at, blocks, stride=8), :], LANES - 3 * channels, 1)
            asked = jnp.where(block == 0, 0.0, pltpu.roll(asked, 1, 0))
            back_tails[pl.ds(1 + at, blocks, stride=8), :] = asked
        from_lane = lax.broadcasted_iota(jnp.int32, (LANES, LANES), 0)
        to_lane = lax.broadcasted_iota(jnp.int32, (LANES, LANES), 1)
        known = lax.broadcasted_iota(jnp.int32, (blocks, LANES), 1) < channels
        spread = jnp.zeros((blocks, LANES), f32)
        for token in range(2):
            gated = jnp.where(known, shorts[0][token] * shorts[1][token], 0.0)
            place = jnp.where(to_lane == 2 * from_lane + token, 1.0, 0.0).astype(bf16)
            for part in halves(gated):
                spread = spread + dot(part, place)
        starts[...] = jnp.zeros((SIDE, LANES), f32)
        starts[pl.ds(0, blocks, stride=per_block), :] = spread

    gated_starts()

    cos, sin = twist[0], twist[1]

    def store_halves(ref, at, value):
        high, low = halves(value)
        ref[at * SIDE : (at + 1) * SIDE, : 2 * SIDE] = high
        ref[at * SIDE : (at + 1) * SIDE, 2 * SIDE :] = low

    def table_right(ref, table, used=WIDE):
        rows = used * SIDE
        return dot(ref[:rows], table[: 4 * SIDE]) + dot(ref[:rows, : 2 * SIDE], table[4 * SIDE :])

    lane = lax.broadcasted_iota(jnp.int32, (SIDE, LANES), 1)
    is_start = (lax.broadcasted_iota(jnp.int32, (SIDE, LANES), 0) % per_block == 0) & (lane < 2)

    def load(n, group):
        level = pltpu.roll(levels[...], LANES - channels - WIDE * n, 1) * (1.0 / CODE_TOP)
        at = WIDE * (n - group * slots)
        values = []
        for i in range(WIDE):
            code = signals[group][pl.ds(at + i, SIDE, stride=GROUP_SIZE), :]
            value = decode(code, level[:, i : i + 1])
            start = pltpu.roll(starts[...], (LANES - 2 * (WIDE * n + i)) % LANES, 1)
            values.append(jnp.where(is_start, start, value))
        return values

    def first_side(values, n):
        for pair in range(len(values) // 2):
            high, low = halves(jnp.concatenate(values[2 * pair : 2 * pair + 2], axis=1))
            both = jnp.concatenate([high, low], axis=0)
            first_raw[n % 2, pair] = dot(first[: 2 * SIDE], both) + dot(first[2 * SIDE :, :SIDE], high)

    def turn(n, used=WIDE):
        for at in range(used):
            span = slice(at % 2 * SIDE, (at % 2 + 1) * SIDE)
            re, im = first_raw[n % 2, at // 2, :SIDE, span], first_raw[n % 2, at // 2, SIDE:, span]
            store_halves(
                turned.at[n % 2], at, jnp.concatenate([re * cos + im * sin, im * cos - re * sin], axis=1)
            )

    def filter_spectrum(n, spectrum):
        of_taps = spectra[WIDE * n // GROUP_SIZE]
        f_re, f_im = of_taps[:, :SIDE], of_taps[:, SIDE:]
        for at in range(WIDE):
            s_re = spectrum[at * SIDE : (at + 1) * SIDE, :SIDE]
            s_im = spectrum[at * SIDE : (at + 1) * SIDE, SIDE:]
            store_halves(
                filtered.at[n % 2],
                at,
                jnp.concatenate([s_re * f_re - s_im * f_im, s_re * f_im + s_im * f_re], axis=1),
            )

    def turn_back(n):
        for at in range(WIDE):
            re = third_raw[n % 2, at * SIDE : (at + 1) * SIDE, :SIDE]
            im = third_raw[n % 2, at * SIDE : (at + 1) * SIDE, SIDE:]
            high, low = halves(jnp.concatenate([re * cos - im * sin, im * cos + re * sin], axis=0))
            unturned[n % 2, : 2 * SIDE, at * SIDE : (at + 1) * SIDE] = high
            unturned[n % 2, 2 * SIDE :, at * SIDE : (at + 1) * SIDE] = low

    def first_side_back(n):
        for pair in range(WIDE // 2):
            span = slice(2 * pair * SIDE, (2 * pair + 2) * SIDE)
            done = dot(fourth[...], unturned[n % 2, : 2 * SIDE, span])
            fourth_raw[n % 2, pair] = (
                done[:SIDE] + done[SIDE:] + dot(fourth[:SIDE], unturned[n % 2, 2 * SIDE :, span])
            )

    def finish(n, group):
        for i in range(WIDE):
            value = fourth_raw[n % 2, i // 2, :, i % 2 * SIDE : (i % 2 + 1) * SIDE]
            top = jnp.max(jnp.max(jnp.abs(value), axis=0, keepdims=True), axis=1, keepdims=True)
            scale = code_scale(top)
            channel = WIDE * n + i
            units[pl.ds(channel, 1), :] = jnp.broadcast_to(scale, (1, LANES))
            place = pl.ds(channel - group * GROUP_SIZE, SIDE, stride=GROUP_SIZE)
            results[group][place, :] = encode(value, CODE_TOP / scale)

    def step(n, load_group, finish_group, active=(True,) * LAGS):
        loads, turns, filters, filtered_back, turns_back, sides_back, finishes = active
        if finishes:
            finish(n - 6, finish_group)
        if sides_back:
            first_side_back(n - 5)
        if turns_back:
            turn_back(n - 4)
        if filters:
            spectrum = table_right(turned.at[n % 2], second)
        if turns:
            turn(n - 1)
        if filtered_back:
            third_raw[(n - 3) % 2] = table_right(filtered.at[(n - 3) % 2], third)
        if filters:
            filter_spectrum(n - 2, spectrum)
        if loads:
            first_side(load(n, load_group), n)

    def pack(slot, half):
        group, above = half // 2, half % 2 * 8
        for i in range(slot_blocks):
            j = slot * slot_blocks + i
            for a in range(per_block):
                at = a * channels + group * GROUP_SIZE + above
                place = (j * per_block + a) * GROUP_SIZE + above
                code = results[group][place : place + 8, :]
                out_ref[j, at : at + 8, :] = code.astype(bf16)

    first_side([taps[pl.ds(g, SIDE, stride=groups), :] for g in range(groups)], -1)
    turn(-1, groups)
    spectra[...] = table_right(turned.at[1], second, groups).reshape(groups, SIDE, 2 * SIDE) * (
        1.0 / (SIDE * SIDE)
    )
    for n in range(LAGS - 1):
        step(n, n // slots, 0, tuple(n >= lag for lag in range(LAGS)))
        if n < slots:
            unpack(n, 1)

    for n in range(LAGS - 1, count):
        step(n, 1, 0)
    for n in range(count, count + LAGS - 1):
        step(n, 1, (n - 6) // slots, tuple(n - lag < count for lag in range(LAGS)))
        for slot in range(slots // 2):
            pack((n - count) % 2 * (slots // 2) + slot, (n - count) // 2)

    diagonal = lax.broadcasted_iota(jnp.int32, (channels, LANES), 1) == lax.broadcasted_iota(
        jnp.int32, (channels, LANES), 0
    )
    scale_row = jnp.sum(jnp.where(diagonal, units[...], 0.0), axis=0, keepdims=True)
    back_tails[pl.ds(0, blocks, stride=8), :] = jnp.broadcast_to(scale_row, (blocks, LANES))
    back_tails[pl.ds(7, blocks, stride=8), :] = jnp.zeros((blocks, LANES), f32)
    out_ref[:, data : data + 8, :] = back_tails[...].reshape(blocks, 8, LANES).astype(bf16)
    for slot in range(slots):
        pack(slot, 2 * groups - 1)
        out_copy(slot).start()
    for slot in range(slots):
        out_copy(slot).wait()


def local_kernel(q_ref, k_ref, v_ref, w_ref, skip_ref, q_out, s_out, ends_out, pads):
    rows, channels = q_ref.shape

    def column(block, carry):
        lanes = pl.ds(pl.multiple_of(block * LANES, LANES), LANES)
        for step in range(rows // SIDE):
            shorts = []
            for at, ref in enumerate((q_ref, k_ref, v_ref)):
                if step == 0:
                    before = jnp.zeros((8, LANES), f32)
                else:
                    before = ref[step * SIDE - 16 : step * SIDE, lanes].astype(f32)[8:]
                shorts.append(
                    short_conv(ref, step * SIDE, lanes, before, w_ref[at, :, lanes], pads.at[at])
                )
            if step == 0:
                ends_out[0:2, lanes] = shorts[1][0:2]
                ends_out[2:4, lanes] = shorts[2][0:2]
            span = slice(step * SIDE, (step + 1) * SIDE)
            q_out[span, lanes] = shorts[0]
            s_out[span, lanes] = skip_ref[:, lanes] * (shorts[1] * shorts[2])
        return carry

    ends_out[...] = jnp.zeros_like(ends_out)
    lax.fori_loop(0, channels // LANES, column, 0)


def join_kernel(
    in_ref, q_ref, s_ref, ends_ref, w_ref, skip_ref, out_hbm, out_buf, units, fixes, sems
):
    rows, channels = q_ref.shape
    blocks = channels // LANES
    sources = in_ref.shape[0] // blocks
    per = LANES // sources
    steps = rows // SIDE
    base = steps * per
    lane = lax.broadcasted_iota(jnp.int32, (8, LANES), 1)
    for block in range(blocks):
        lanes = slice(block * LANES, (block + 1) * LANES)
        tail = jnp.zeros((8, LANES), f32)
        for i in range(sources):
            part = in_ref[block * sources + i, base : base + 8, :].astype(f32)
            tail = jnp.where(lane // per == i, pltpu.roll(part, i * per, 1), tail)
        units[:, lanes] = tail[0:1] * (1.0 / CODE_TOP)
        adds = []
        for at in range(3):
            ago_2, ago_1 = tail[1 + 2 * at : 2 + 2 * at], tail[2 + 2 * at : 3 + 2 * at]
            weight_1, weight_2 = w_ref[at, 1:2, lanes], w_ref[at, 2:3, lanes]
            adds.append((weight_1 * ago_1 + weight_2 * ago_2, weight_2 * ago_1))
        for token in range(2):
            k_short = ends_ref[token : token + 1, lanes] + adds[1][token]
            v_short = ends_ref[2 + token : 3 + token, lanes] + adds[2][token]
            fixes[token : token + 1, lanes] = q_ref[token : token + 1, lanes] + adds[0][token]
            fixes[2 + token : 3 + token, lanes] = skip_ref[:, lanes] * (k_short * v_short)

    first_rows = lax.broadcasted_iota(jnp.int32, (8, LANES), 0) < 2
    copies = []
    for step in range(steps):
        span = slice(step * SIDE, (step + 1) * SIDE)

        for block in range(blocks):
            lanes = slice(block * LANES, (block + 1) * LANES)
            of_block = slice(block * sources, (block + 1) * sources)
            code = in_ref[of_block, step * per : (step + 1) * per, :]
            tile = code.astype(f32).reshape(LANES, SIDE).T
            long_conv = decode(tile, units[:, lanes])
            q_short, skipped = q_ref[span, lanes], s_ref[span, lanes]
            if step == 0:
                fix = fixes[:, lanes]
                q_start = jnp.where(first_rows, fix, q_short[:8])
                s_start = jnp.where(first_rows, pltpu.roll(fix, 6, 0), skipped[:8])
                q_short = jnp.concatenate([q_start, q_short[8:]], axis=0)
                skipped = jnp.concatenate([s_start, skipped[8:]], axis=0)
            out_buf[span, lanes] = (q_short * (long_conv + skipped)).astype(bf16)
        rows_at = pl.ds(step * SIDE, SIDE)
        copies.append(
            pltpu.make_async_copy(out_buf.at[rows_at], out_hbm.at[rows_at], sems.at[step])
        )
        copies[-1].start()
    for copy in copies:
        copy.wait()


def shards(query_in, key_in, value_in, short_weight, skip_bias, filter_taps):
    rows, channels = query_in.shape
    seq = lax.axis_size("seq")
    own = channels // seq
    blocks = channels // LANES
    groups = own // GROUP_SIZE
    sent = rows * own // LANES
    steps = rows // SIDE
    whole = pl.BlockSpec(memory_space=pltpu.VMEM)
    hbm = pl.BlockSpec(memory_space=pltpu.HBM)
    resident = pltpu.CompilerParams(vmem_limit_bytes=RESIDENT_LIMIT)
    streaming = pltpu.CompilerParams(vmem_limit_bytes=STREAMING_LIMIT)

    message = pl.pallas_call(
        gate_kernel,
        in_specs=[hbm] * 5,
        out_specs=hbm,
        out_shape=jax.ShapeDtypeStruct((seq, sent + 16, LANES), bf16),
        scratch_shapes=[
            pltpu.VMEM((rows, channels), bf16),
            pltpu.VMEM((rows, channels), bf16),
            pltpu.VMEM((16, channels), bf16),
            pltpu.VMEM(short_weight.shape, f32),
            pltpu.VMEM(filter_taps.shape, f32),
            pltpu.VMEM((seq, sent + 16, LANES), bf16),
            pltpu.VMEM((blocks, 2, 16 + SIDE, LANES), f32),
            pltpu.VMEM((8, channels), f32),
            pltpu.VMEM((blocks, 8, LANES), f32),
            pltpu.VMEM((blocks, 8, LANES), f32),
            pltpu.VMEM((blocks + 1, 2 * steps * filter_taps.shape[0] // blocks, LANES), f32),
            pltpu.SemaphoreType.DMA((4, steps)),
            pltpu.SemaphoreType.DMA((blocks,)),
        ],
        compiler_params=streaming,
        name="gate",
    )(query_in, key_in, value_in, short_weight, filter_taps)
    message, query_in, key_in, value_in, short_weight, skip_bias, known = lax.optimization_barrier(
        (message, query_in, key_in, value_in, short_weight, skip_bias, table_blocks())
    )
    message = lax.all_to_all(message, "seq", 0, 0)

    q_short, skipped, ends = pl.pallas_call(
        local_kernel,
        in_specs=[whole] * 5,
        out_specs=[whole] * 3,
        out_shape=[
            jax.ShapeDtypeStruct((rows, channels), f32),
            jax.ShapeDtypeStruct((rows, channels), f32),
            jax.ShapeDtypeStruct((8, channels), f32),
        ],
        scratch_shapes=[pltpu.VMEM((3, 16 + SIDE, LANES), f32)],
        compiler_params=streaming,
        cost_estimate=pl.CostEstimate(
            flops=20 * rows * channels, bytes_accessed=14 * rows * channels, transcendentals=0
        ),
        name="local",
    )(query_in, key_in, value_in, short_weight, skip_bias[None])
    weights = lax.dynamic_slice_in_dim(short_weight, lax.axis_index("seq") * own, own, axis=2)
    weights = jnp.pad(weights, ((0, 0), (0, 0), (0, LANES - own)))
    message, q_short, skipped, ends, weights = lax.optimization_barrier(
        (message, q_short, skipped, ends, weights)
    )

    message = pl.pallas_call(
        mix_kernel,
        in_specs=[whole] * 3,
        out_specs=hbm,
        out_shape=jax.ShapeDtypeStruct((seq, sent + 8, LANES), bf16),
        scratch_shapes=[
            pltpu.VMEM((seq, sent + 8, LANES), bf16),
            *[pltpu.VMEM((seq * sent // groups, LANES), f32)] * (2 * groups),
            pltpu.VMEM((seq * 8, LANES), f32),
            pltpu.VMEM((groups, SIDE, 2 * SIDE), f32),
            pltpu.VMEM((own, LANES), f32),
            pltpu.VMEM((seq * 8, LANES), f32),
            pltpu.VMEM((seq * 8, LANES), f32),
            pltpu.VMEM((SIDE, LANES), f32),
            pltpu.VMEM((SIDE, LANES), f32),
            pltpu.VMEM((2, WIDE * SIDE, 4 * SIDE), bf16),
            pltpu.VMEM((2, WIDE * SIDE, 4 * SIDE), bf16),
            pltpu.VMEM((2, 4 * SIDE, WIDE * SIDE), bf16),
            pltpu.VMEM((2, WIDE // 2, 2 * SIDE, 2 * SIDE), f32),
            pltpu.VMEM((2, WIDE * SIDE, 2 * SIDE), f32),
            pltpu.VMEM((2, WIDE // 2, SIDE, 2 * SIDE), f32),
            pltpu.VMEM((4 * SIDE, 2 * SIDE), bf16),
            pltpu.VMEM((6 * SIDE, 2 * SIDE), bf16),
            pltpu.VMEM((6 * SIDE, 2 * SIDE), bf16),
            pltpu.VMEM((2 * SIDE, 2 * SIDE), bf16),
            pltpu.VMEM((2, SIDE, LANES), f32),
            pltpu.SemaphoreType.DMA((own // WIDE // groups,)),
        ],
        compiler_params=pltpu.CompilerParams(vmem_limit_bytes=MIX_LIMIT),
        name="mix",
    )(message, weights, known)
    message = lax.all_to_all(message, "seq", 0, 0)

    return pl.pallas_call(
        join_kernel,
        in_specs=[whole] * 6,
        out_specs=hbm,
        out_shape=jax.ShapeDtypeStruct((rows, channels), bf16),
        scratch_shapes=[
            pltpu.VMEM((rows, channels), bf16),
            pltpu.VMEM((1, channels), f32),
            pltpu.VMEM((8, channels), f32),
            pltpu.SemaphoreType.DMA((steps,)),
        ],
        compiler_params=resident,
        name="join",
    )(message, q_short, skipped, ends, short_weight, skip_bias[None])


def solution(mesh):
    in_specs = (
        P("seq", "ch"),
        P("seq", "ch"),
        P("seq", "ch"),
        P(None, None, "ch"),
        P("ch"),
        P("ch", "seq"),
    )
    out_specs = P("seq", "ch")
    return jax.shard_map(shards, mesh=mesh, in_specs=in_specs, out_specs=out_specs, check_vma=False)
```
